256 devices in a mesh: col: 64 (over z, x, core), rep: 4 (over y).
Axes of the slice: x: 4, y: 4, z: 8, core: 2. Of those that a mesh axis runs over, the one named last changes fastest.
Arguments:
- looked: bfloat16 [32768, 1024], P('rep', 'col'), may hold values from -6 to 6
- cotangent: bfloat16 [32768, 1024], P('rep', 'col'), may hold values from -16 to 16
- w_in: bfloat16 [1024, 4096], replicated, may hold values from -0.1875 to 0.1875
- w_out: bfloat16 [1024, 1024], replicated, may hold values from -0.1875 to 0.1875
- lengths: int32 [512], P('rep'), may hold values from 1 to 127, as said below
- owner: int32 [512], P('rep'), may hold values from 0 to 63, as said below
Outputs:
- d_looked: bfloat16 [32768, 1024], P('rep', 'col')
- d_w_out: float32 [1024, 1024], P('col')
The draws below stay inside these ranges and needn't reach their ends.
Inputs may be any that keep to these rules, and one draw needn't show every extreme that they name: In each replica group's 128 users every owner appears exactly 2 times, and the lengths of an owner's users sum to exactly 128. The lengths of one replica group's users sum to 8192.
All inputs are finite; a program needn't handle non-finite values.
Results may differ from the reference program's by a relative error of at most 0.018.
Values may be sent and summed in bfloat16 or wider, within the bound.
No kernel may reach another device: no remote copies, remote signals or barrier semaphores. Data moves between devices by JAX's collectives and lax.ppermute only.
A program may use at most 64 MiB of HBM per device.

```python
import jax
import jax.numpy as jnp
from jax import lax

D = 1024
HEADS = 8
EV_DEV = 128
U_DEV = 2
EVENTS = 32768
N_COL = 64
N_REP = 4


def routing_draw(key):
    mean_len = EV_DEV // U_DEV
    pairs = U_DEV // 2
    first = jax.random.randint(jax.random.fold_in(key, 11), (N_REP, N_COL, pairs), 1, 2 * mean_len)
    forced = jax.random.randint(jax.random.fold_in(key, 12), (N_REP, 1, 1), 0, N_COL)
    col_ids = jnp.arange(N_COL, dtype=jnp.int32)[None, :, None]
    pair_ids = jnp.arange(pairs, dtype=jnp.int32)[None, None, :]
    first = jnp.where((col_ids == forced) & (pair_ids == 0), 2 * mean_len - 1, first)
    group_lens = jnp.concatenate([first, 2 * mean_len - first], axis=2).reshape(N_REP, N_COL * U_DEV)
    owners = jnp.broadcast_to(jnp.arange(N_COL, dtype=jnp.int32)[:, None], (N_COL, U_DEV)).reshape(N_COL * U_DEV)
    group_keys = jax.random.split(jax.random.fold_in(key, 13), N_REP)
    order = jax.vmap(lambda one: jax.random.permutation(one, N_COL * U_DEV))(group_keys)
    shuffled = jnp.take_along_axis(group_lens, order, axis=1).reshape(-1)
    assigned = owners[order].reshape(-1)
    return (shuffled.astype(jnp.int32), assigned.astype(jnp.int32))


def draw_lengths(key, part):
    return routing_draw(key)[0]


def draw_owner(key, part):
    return routing_draw(key)[1]


def spiked(drawn, key, source, target, blocks, factor):
    owner, partner = [(jnp.arange(drawn.shape[axis_at]) // (drawn.shape[axis_at] // blocks)).reshape([-1 if axis == axis_at else 1 for axis in range(drawn.ndim)]) for axis_at in (source, target)]
    chosen = jax.random.permutation(key, blocks)[partner]
    strong = (owner == chosen) | (owner == (partner + blocks // 2) % blocks)
    return jnp.where(strong, factor * drawn, drawn)


def steps_of(own_key, dims, cuts, least, top_value):
    factor_of, own = 1.0, jax.random.fold_in(own_key, 6)
    for dim, blocks in cuts:
        draws = jnp.exp(jax.random.uniform(jax.random.fold_in(own, dim), (blocks,), jnp.float32, least / len(cuts), top_value / len(cuts)))
        factor_of = factor_of * jnp.repeat(draws, dims[dim] // blocks).reshape([-1 if axis == dim else 1 for axis in range(len(dims))])
    return factor_of


def bell_draw(own_key, extent, scale, bound, cuts=(), kind=jnp.bfloat16):
    gain = steps_of(own_key, extent, cuts, -0.22, 0.18) if cuts else 1.0
    drawn = jax.random.normal(own_key, extent, jnp.float32) * scale * gain
    return jnp.minimum(jnp.maximum(drawn, -bound), bound).astype(kind)


def heavy_noise(own_key, extent, scale, bound, cuts, heavy, held_as=jnp.bfloat16):
    values = scale * jax.random.normal(own_key, extent, jnp.float32)
    if cuts:
        values = values * steps_of(own_key, extent, cuts, -0.22, 0.18)
    return jnp.clip(spiked(values, jax.random.fold_in(own_key, 3), *heavy), -bound, bound).astype(held_as)


def setup_inputs(seed: int = 0) -> dict:
    seeds = jax.random.split(jax.random.key(seed), 7)
    return {
        "looked": bell_draw(seeds[0], (EVENTS, D), 1.0, 6.0, ((0, 4), (1, 64))),
        "cotangent": heavy_noise(seeds[1], (EVENTS, D), 1.0, 16.0, ((0, 4), (1, 64)), (0, 1, 64, 4.0)),
        "w_in": bell_draw(seeds[2], (D, 4 * D), D ** -0.5, 0.1875),
        "w_out": bell_draw(seeds[3], (D, D), D ** -0.5, 0.1875),
        "lengths": draw_lengths(jax.random.fold_in(seeds[6], 71), 0),
        "owner": draw_owner(jax.random.fold_in(seeds[6], 71), 0),
    }


EPS = 1e-05

def layer_norm(values):
    center = values - lax.optimization_barrier(jnp.mean(values, axis=-1, keepdims=True))
    return center * lax.rsqrt(lax.optimization_barrier(jnp.mean(center * center, axis=-1, keepdims=True)) + EPS)

def hstu_layer(rows, w_in, w_out, allowed):
    count = rows.shape[0]
    width = rows.shape[1]
    normed = layer_norm(rows.astype(jnp.float32)).astype(rows.dtype)
    acts = jax.nn.silu(jnp.dot(normed, w_in, preferred_element_type=jnp.float32)).astype(rows.dtype)
    gates = acts[:, :width]
    values = acts[:, width:2 * width].reshape(count, HEADS, -1).astype(jnp.float32)
    queries = acts[:, 2 * width:3 * width].reshape(count, HEADS, -1).astype(jnp.float32)
    keys = acts[:, 3 * width:].reshape(count, HEADS, -1).astype(jnp.float32)
    scale = 1.0 / jnp.sqrt(jnp.float32(queries.shape[2]))
    scores = jnp.einsum('qhd,khd->hqk', queries, keys) * scale
    weights = jnp.where(allowed[None], jax.nn.silu(scores), 0.0).astype(rows.dtype)
    attended = jnp.einsum('hqk,khd->qhd', weights.astype(jnp.float32), values).reshape(count, width)
    mixed = (layer_norm(attended) * gates.astype(jnp.float32)).astype(rows.dtype)
    output = rows.astype(jnp.float32) + jnp.dot(mixed, w_out, preferred_element_type=jnp.float32)
    return (output, mixed)

def prepare(rows, segment, w_in, w_out):
    position = jnp.arange(rows.shape[0], dtype=jnp.int32)
    allowed = (segment[:, None] == segment[None, :]) & (position[None, :] <= position[:, None])

    def forward(inputs):
        return hstu_layer(inputs, w_in, w_out, allowed)
    output, pullback, mixed = jax.vjp(forward, rows, has_aux=True)
    return (output, pullback, mixed)

def routing(lengths, owner, count_cols, cap):
    users = lengths.shape[0]
    total = count_cols * cap
    ends = jnp.cumsum(lengths).astype(jnp.int32)
    offsets = (ends - lengths).astype(jnp.int32)
    onehot = (owner[:, None] == jnp.arange(count_cols, dtype=jnp.int32)[None, :]).astype(jnp.int32)
    loads = onehot * lengths[:, None]
    before = (jnp.cumsum(loads, axis=0).astype(jnp.int32) - loads).astype(jnp.int32)
    start = lax.optimization_barrier(jnp.sum(before * onehot, axis=1)).astype(jnp.int32)
    user_of = jnp.repeat(jnp.arange(users, dtype=jnp.int32), lengths, total_repeat_length=total).astype(jnp.int32)
    inside = (jnp.arange(total, dtype=jnp.int32) - offsets[user_of]).astype(jnp.int32)
    flat = (owner[user_of] * cap + start[user_of] + inside).astype(jnp.int32)
    inverse = jnp.zeros((total,), jnp.int32).at[flat].set(jnp.arange(total, dtype=jnp.int32))
    return (flat, inverse, user_of)

def reference(looked, cotangent, w_in, w_out, lengths, owner):
    width = looked.shape[1]
    cap = EV_DEV
    group_events = EV_DEV * N_COL
    group_users = U_DEV * N_COL
    pieces = []
    total_grad = jnp.zeros((width, width), jnp.float32)
    for group in range(N_REP):
        rows = looked[group * group_events:(group + 1) * group_events]
        cots = cotangent[group * group_events:(group + 1) * group_events]
        lens = lengths[group * group_users:(group + 1) * group_users]
        owns = owner[group * group_users:(group + 1) * group_users]
        flat, inverse, user_of = routing(lens, owns, N_COL, cap)
        packed = rows[inverse].reshape(N_COL, cap, width)
        packed_cot = cots[inverse].reshape(N_COL, cap, width)
        segment = user_of[inverse].reshape(N_COL, cap)

        def per_owner(carry, item):
            block, block_cot, block_seg = item
            output, pullback, mixed = prepare(block, block_seg, w_in, w_out)
            grad_rows = pullback(block_cot.astype(output.dtype))[0]
            term = lax.dot_general(mixed, block_cot, (((0,), (0,)), ((), ())), preferred_element_type=jnp.float32)
            return (carry + term, grad_rows)
        total_grad, grads = lax.scan(per_owner, total_grad, (packed, packed_cot, segment))
        pieces.append(grads.reshape(group_events, width)[flat])
    return (jnp.concatenate(pieces, axis=0), total_grad)
```

```python
import functools

import jax
import jax.numpy as jnp
from jax import lax
from jax.experimental import pallas as pl
from jax.experimental.pallas import tpu as pltpu
from jax.sharding import PartitionSpec as P

HEADS = 8
EPS = 1e-05
BF = jnp.bfloat16
F32 = jnp.float32
LANES = 128
WEIGHT_CHUNKS = 8

SMEM = pl.BlockSpec(memory_space=pltpu.SMEM)
VMEM = pl.BlockSpec(memory_space=pltpu.VMEM)
ANY = pl.BlockSpec(memory_space=pl.ANY)


def params(mib):
    return pltpu.CompilerParams(vmem_limit_bytes=mib << 20)


def shape(dims, dtype=BF):
    return jax.ShapeDtypeStruct(dims, dtype)


def dot(a, b, ca, cb):
    return lax.dot_general(a, b, (((ca,), (cb,)), ((), ())), preferred_element_type=F32)


def pack_kernel(len_ref, own_ref, me_ref, x_ref, c_ref, out_ref, off_ref, start_ref, mine_ref, tab, seen):
    users = len_ref.shape[0]
    owners = users // 2
    last = x_ref.shape[1] - LANES

    def clear(j, carry):
        seen[j] = 0
        return carry

    lax.fori_loop(0, owners, clear, 0, unroll=8)

    def user(u, off):
        own = own_ref[u]
        length = len_ref[u]
        second = seen[own]
        seen[own] = 1
        start = second * (LANES - length)
        off_ref[u] = off
        start_ref[u] = start
        tab[second, own] = off - start
        tab[2 + second, own] = length
        return off + length

    lax.fori_loop(0, users, user, 0, unroll=4)
    mine_ref[0] = tab[2, me_ref[0]]
    lane = lax.broadcasted_iota(jnp.int32, (16, LANES), 1)

    def owner(j, carry):
        both = []
        for k in range(2):
            first = tab[k, j]
            base = pl.multiple_of((first // LANES) * LANES, LANES)
            after = pl.multiple_of(jnp.minimum(base + LANES, last), LANES)
            inside = first % LANES
            back = (LANES - inside) % LANES
            low = lane >= inside
            both.append(
                [
                    pltpu.roll(jnp.where(low, ref[:, pl.ds(base, LANES)], ref[:, pl.ds(after, LANES)]), back, 1)
                    for ref in (x_ref, c_ref)
                ]
            )
        head = lane < tab[2, j]
        out_ref[j, 0:16, :] = jnp.where(head, both[0][0], both[1][0])
        out_ref[j, 16:32, :] = jnp.where(head, both[0][1], both[1][1])
        return carry

    lax.fori_loop(0, owners, owner, 0, unroll=4)


def unpack_kernel(len_ref, own_ref, off_ref, start_ref, g_ref, out_ref, wide):
    users = len_ref.shape[0]
    lane = lax.broadcasted_iota(jnp.int32, (16, LANES), 1)

    def user(u, carry):
        off = off_ref[u]
        length = len_ref[u]
        base = pl.multiple_of((off // LANES) * LANES, LANES)
        inside = off % LANES
        turn = (inside - start_ref[u]) % LANES
        moved = pltpu.roll(g_ref[own_ref[u]], turn, 1).astype(F32)
        end = inside + length
        pltpu.store(wide.at[:, pl.ds(base, LANES)], moved, mask=(lane >= inside) & (lane < end))
        pltpu.store(wide.at[:, pl.ds(base + LANES, LANES)], moved, mask=lane < end - LANES)
        return carry

    lax.fori_loop(0, users, user, 0, unroll=8)
    out_ref[...] = wide[:, : out_ref.shape[1]].astype(BF)


def sigmoid(v):
    return 0.5 * jnp.tanh(0.5 * v) + 0.5


def norm_parts(v):
    center = v - jnp.mean(v, axis=-1, keepdims=True)
    rstd = lax.rsqrt(jnp.mean(center * center, axis=-1, keepdims=True) + EPS)
    return center * rstd, rstd


def norm_back(hat, rstd, d):
    return rstd * (d - jnp.mean(d, axis=-1, keepdims=True) - hat * jnp.mean(d * hat, axis=-1, keepdims=True))


def forward_kernel(mine_ref, rc_ref, w_in_hbm, acts_ref, slope_ref, wts_ref, wslope_ref, ahat_ref, arstd_ref, mixed_t_ref, w_in, sems):
    width = rc_ref.shape[0] * 16
    rows = rc_ref.shape[2]
    per = w_in.shape[1] // WEIGHT_CHUNKS

    def fetch(i):
        part = pl.ds(i * per, per)
        return pltpu.make_async_copy(w_in_hbm.at[:, part], w_in.at[:, part], sems.at[i])

    order = [2, 3, 4, 5, 6, 7, 0, 1]
    for i in order:
        fetch(i).start()
    x = rc_ref[:, 0:16, :].reshape(width, rows).T
    normed = norm_parts(x.astype(F32))[0].astype(BF)
    for i in order:
        fetch(i).wait()
        part = slice(i * per, (i + 1) * per)
        pre = dot(normed, w_in[:, part], 1, 0)
        gate = sigmoid(pre)
        act = pre * gate
        acts_ref[:, part] = act.astype(BF)
        slope_ref[:, part] = (gate + act * (1.0 - gate)).astype(BF)
    query = lax.broadcasted_iota(jnp.int32, (rows, rows), 0)
    key = lax.broadcasted_iota(jnp.int32, (rows, rows), 1)
    first = mine_ref[0]
    allowed = ((query < first) == (key < first)) & (key <= query)
    each = width // HEADS
    scale = float(each) ** -0.5
    attended = []
    for h in range(HEADS):
        v = acts_ref[:, width + h * each : width + (h + 1) * each]
        q = acts_ref[:, 2 * width + h * each : 2 * width + (h + 1) * each]
        k = acts_ref[:, 3 * width + h * each : 3 * width + (h + 1) * each]
        scores = dot(q, k, 1, 1) * scale
        gate = sigmoid(scores)
        weight = scores * gate
        kept = jnp.where(allowed, weight, 0.0).astype(BF)
        wts_ref[h] = kept
        wslope_ref[h] = jnp.where(allowed, (gate + weight * (1.0 - gate)) * scale, 0.0).astype(BF)
        attended.append(dot(kept, v, 1, 0))
    hat, rstd = norm_parts(jnp.concatenate(attended, axis=1))
    ahat_ref[...] = hat
    arstd_ref[...] = jnp.broadcast_to(rstd, arstd_ref.shape)
    mixed_t_ref[...] = (hat * acts_ref[:, :width].astype(F32)).astype(BF).T


def product_kernel(pos_ref, mixed_t_ref, rc_ref, send_ref, keep_ref, cots):
    core, y = pos_ref[0], pos_ref[1]
    cots[...] = rc_ref[:, 16:32, :].reshape(cots.shape)
    rows = mixed_t_ref[...].reshape(32, 2, 16, LANES)
    quarter = cots.shape[0] // 4
    flip, mirror = y ^ 1, 3 - y
    slots = ((flip, 3 - flip, mirror, y), (mirror, mirror ^ 1, flip, y))
    for side in range(2):
        picked = rows[:, side].reshape(512, LANES)
        for half in range(2):
            part = picked[half * 256 : (half + 1) * 256]
            for s in range(4):
                cols = cots[pl.ds(pl.multiple_of(slots[half][s] * quarter, quarter), quarter), :]
                term = dot(part, cols, 1, 1).astype(BF)

                @pl.when(core == side)
                def _():
                    keep_ref[half, s] = term

                @pl.when(core != side)
                def _():
                    send_ref[half, s] = term


def backward_kernel(rc_ref, acts_ref, slope_ref, wts_ref, wslope_ref, ahat_ref, arstd_ref, w_in_hbm, w_out_ref, grad_ref, w_in, d_pre, sems):
    width = rc_ref.shape[0] * 16
    rows = rc_ref.shape[2]
    per = w_in.shape[1] // WEIGHT_CHUNKS

    def fetch(i):
        part = pl.ds(i * per, per)
        return pltpu.make_async_copy(w_in_hbm.at[:, part], w_in.at[:, part], sems.at[i])

    for i in range(WEIGHT_CHUNKS):
        fetch(i).start()
    cots = rc_ref[:, 16:32, :].reshape(width, rows).T
    d_mixed = dot(cots, w_out_ref[...], 1, 1).astype(BF).astype(F32)
    hat = ahat_ref[...]
    d_pre[:, :width] = ((d_mixed * hat) * slope_ref[:, :width].astype(F32)).astype(BF)
    d_att = norm_back(hat, arstd_ref[:, 0:1], d_mixed * acts_ref[:, :width].astype(F32)).astype(BF)
    each = width // HEADS
    for h in range(HEADS):
        vs = slice(width + h * each, width + (h + 1) * each)
        qs = slice(2 * width + h * each, 2 * width + (h + 1) * each)
        ks = slice(3 * width + h * each, 3 * width + (h + 1) * each)
        da = d_att[:, h * each : (h + 1) * each]
        d_weight = dot(da, acts_ref[:, vs], 1, 1)
        d_score = (d_weight * wslope_ref[h].astype(F32)).astype(BF)
        d_pre[:, vs] = (dot(wts_ref[h], da, 0, 0) * slope_ref[:, vs].astype(F32)).astype(BF)
        d_pre[:, qs] = (dot(d_score, acts_ref[:, ks], 1, 0) * slope_ref[:, qs].astype(F32)).astype(BF)
        d_pre[:, ks] = (dot(d_score, acts_ref[:, qs], 0, 0) * slope_ref[:, ks].astype(F32)).astype(BF)
    d_normed = jnp.zeros((rows, width), F32)
    for i in range(WEIGHT_CHUNKS):
        fetch(i).wait()
        part = slice(i * per, (i + 1) * per)
        d_normed += dot(d_pre[:, part], w_in[:, part], 1, 1)
    x = rc_ref[:, 0:16, :].reshape(width, rows).T
    normed, rstd = norm_parts(x.astype(F32))
    grad = norm_back(normed, rstd, d_normed) + cots.astype(F32)
    grad_ref[...] = grad.astype(BF).T.reshape(grad_ref.shape)


def core_sum_kernel(keep_ref, got_ref, a1_ref, b1_ref, rest_ref):
    for half, out in ((0, a1_ref), (1, b1_ref)):
        for s in range(4):
            total = keep_ref[half, s].astype(F32) + got_ref[half, s].astype(F32)
            if s < 2:
                out[s] = total.astype(BF)
            else:
                rest_ref[half, s - 2] = total.astype(BF)


def first_sum_kernel(rest_ref, ga_ref, gb_ref, a2_ref, b2_ref, own_ref):
    for half, got, out in ((0, ga_ref, a2_ref), (1, gb_ref, b2_ref)):
        out[...] = (rest_ref[half, 0].astype(F32) + got[1].astype(F32)).astype(BF)
        own_ref[half] = (rest_ref[half, 1].astype(F32) + got[0].astype(F32)).astype(BF)


def second_sum_kernel(pos_ref, own_ref, ga_ref, gb_ref, *out_refs):
    x = pos_ref[2]
    for half, got in ((0, ga_ref), (1, gb_ref)):
        total = (own_ref[half].astype(F32) + got[...].astype(F32)).astype(BF).reshape(4, 4, 16, 256)
        for xx in range(4):
            for k in range(4):

                @pl.when((x + k) % 4 == xx)
                def _():
                    out_refs[k][half * 4 : (half + 1) * 4] = total[:, xx]


def x_sum_kernel(pos_ref, *refs):
    z = pos_ref[3]
    parts, outs = refs[:4], refs[4:]
    for k in range(8):
        to = (z + k) % 8
        total = parts[0][to].astype(F32)
        for part in parts[1:]:
            total += part[to].astype(F32)
        outs[k][...] = total.astype(outs[k].dtype)


def z_sum_kernel(*refs):
    total = refs[0][...].astype(F32)
    for part in refs[1:-1]:
        total += part[...].astype(F32)
    refs[-1][...] = total


def join_kernel(pos_ref, *refs):
    y = pos_ref[1]
    for k in range(4):
        at = (y + 4 - k) % 4
        refs[-1][:, pl.ds(pl.multiple_of(at * 256, 256), 256)] = refs[k][...]


def summed(pos, send, keep):
    half = (2, 256, 256)
    got = lax.ppermute(send, "col", [(i, i ^ 1) for i in range(64)])
    a1, b1, rest = pl.pallas_call(
        core_sum_kernel, out_shape=(shape(half), shape(half), shape((2,) + half)), compiler_params=params(32)
    )(keep, got)
    flip = [(i, i ^ 1) for i in range(4)]
    mirror = [(i, 3 - i) for i in range(4)]
    ga, gb = lax.ppermute(a1, "rep", flip), lax.ppermute(b1, "rep", mirror)
    a2, b2, own = pl.pallas_call(
        first_sum_kernel, out_shape=(shape(half[1:]), shape(half[1:]), shape(half)), compiler_params=params(32)
    )(rest, ga, gb)
    ga, gb = lax.ppermute(a2, "rep", mirror), lax.ppermute(b2, "rep", flip)
    parts = pl.pallas_call(
        second_sum_kernel,
        out_shape=[shape((8, 16, 256))] * 4,
        in_specs=[SMEM] + [VMEM] * 3,
        compiler_params=params(32),
    )(pos, own, ga, gb)

    def along_x(k):
        return [((z * 4 + x) * 2 + c, (z * 4 + (x + k) % 4) * 2 + c) for z in range(8) for x in range(4) for c in range(2)]

    def along_z(k):
        return [(z * 8 + r, (z + k) % 8 * 8 + r) for z in range(8) for r in range(8)]

    parts = [parts[0]] + [lax.ppermute(parts[k], "col", along_x(k)) for k in range(1, 4)]
    parts = pl.pallas_call(
        x_sum_kernel,
        out_shape=[shape((16, 256), F32)] + [shape((16, 256))] * 7,
        in_specs=[SMEM] + [VMEM] * 4,
        compiler_params=params(32),
    )(pos, *parts)
    parts = [parts[0]] + [lax.ppermute(parts[k], "col", along_z(k)) for k in range(1, 8)]
    mine = pl.pallas_call(z_sum_kernel, out_shape=shape((16, 256), F32), compiler_params=params(32))(*parts)
    parts = [mine] + [lax.ppermute(mine, "rep", [(i, (i + k) % 4) for i in range(4)]) for k in range(1, 4)]
    return pl.pallas_call(
        join_kernel,
        out_shape=shape((16, 1024), F32),
        in_specs=[SMEM] + [VMEM] * 4,
        compiler_params=params(32),
    )(pos, *parts)


def per_device(looked, cotangent, w_in, w_out, lengths, owner):
    cols = lax.axis_size("col")
    events, mine_cols = looked.shape
    width = w_out.shape[0]
    rows = events // cols
    users = lengths.shape[0]
    me = lax.axis_index("col")
    pos = jnp.stack([me % 2, lax.axis_index("rep"), me // 2 % 4, me // 8]).astype(jnp.int32)
    send, off, start, mine = pl.pallas_call(
        pack_kernel,
        out_shape=(
            shape((cols, 2 * mine_cols, rows)),
            shape((users,), jnp.int32),
            shape((users,), jnp.int32),
            shape((1,), jnp.int32),
        ),
        in_specs=[SMEM, SMEM, SMEM, VMEM, VMEM],
        out_specs=(VMEM, SMEM, SMEM, SMEM),
        scratch_shapes=[pltpu.SMEM((4, cols), jnp.int32), pltpu.SMEM((cols,), jnp.int32)],
        compiler_params=params(32),
    )(lengths, owner, me.reshape(1).astype(jnp.int32), looked.T, cotangent.T)
    packed = lax.all_to_all(send, "col", split_axis=0, concat_axis=0, tiled=True)
    acts, slope, wts, wslope, ahat, arstd, mixed_t = pl.pallas_call(
        forward_kernel,
        out_shape=(
            shape((rows, 4 * width)),
            shape((rows, 4 * width)),
            shape((HEADS, rows, rows)),
            shape((HEADS, rows, rows)),
            shape((rows, width), F32),
            shape((rows, LANES), F32),
            shape((width, rows)),
        ),
        in_specs=[SMEM, VMEM, ANY],
        scratch_shapes=[pltpu.VMEM(w_in.shape, BF), pltpu.SemaphoreType.DMA((WEIGHT_CHUNKS,))],
        compiler_params=params(48),
    )(mine, packed, w_in)
    half = (2, 4, 256, 256)
    p_send, p_keep = pl.pallas_call(
        product_kernel,
        out_shape=(shape(half), shape(half)),
        in_specs=[SMEM, VMEM, VMEM],
        scratch_shapes=[pltpu.VMEM((width, rows), BF)],
        compiler_params=params(32),
    )(pos, mixed_t, packed)
    d_w_out = summed(pos, p_send, p_keep)
    grad = pl.pallas_call(
        backward_kernel,
        out_shape=shape((cols, mine_cols, rows)),
        in_specs=[VMEM] * 7 + [ANY, VMEM],
        scratch_shapes=[
            pltpu.VMEM(w_in.shape, BF),
            pltpu.VMEM((rows, 4 * width), BF),
            pltpu.SemaphoreType.DMA((WEIGHT_CHUNKS,)),
        ],
        compiler_params=params(48),
    )(packed, acts, slope, wts, wslope, ahat, arstd, w_in, w_out)
    back = lax.all_to_all(grad, "col", split_axis=0, concat_axis=0, tiled=True)
    d_looked = pl.pallas_call(
        unpack_kernel,
        out_shape=shape((mine_cols, events)),
        in_specs=[SMEM] * 4 + [VMEM],
        scratch_shapes=[pltpu.VMEM((mine_cols, events + LANES), F32)],
        compiler_params=params(32),
    )(lengths, owner, off, start, back)
    return (d_looked.T, d_w_out)


def solution(mesh):
    placed = (P("rep", "col"), P("rep", "col"), P(), P(), P("rep"), P("rep"))
    return jax.shard_map(
        per_device,
        mesh=mesh,
        in_specs=placed,
        out_specs=(P("rep", "col"), P("col", None)),
        check_vma=False,
    )
```

```python
import functools

import jax
import jax.numpy as jnp
from jax import lax
from jax.experimental import pallas as pl
from jax.experimental.pallas import tpu as pltpu
from jax.sharding import PartitionSpec as P

HEADS = 8
EPS = 1e-05
BF = jnp.bfloat16
F32 = jnp.float32
LANES = 128
WEIGHT_CHUNKS = 8

SMEM = pl.BlockSpec(memory_space=pltpu.SMEM)
VMEM = pl.BlockSpec(memory_space=pltpu.VMEM)
ANY = pl.BlockSpec(memory_space=pl.ANY)


def params(mib):
    return pltpu.CompilerParams(vmem_limit_bytes=mib << 20)


def shape(dims, dtype=BF):
    return jax.ShapeDtypeStruct(dims, dtype)


def dot(a, b, ca, cb):
    return lax.dot_general(a, b, (((ca,), (cb,)), ((), ())), preferred_element_type=F32)


def pack_kernel(len_hbm, own_hbm, me_ref, x_hbm, c_hbm, out_ref, table, lens, owns, x_ref, c_ref, tab, seen, sems):
    copies = [
        pltpu.make_async_copy(src, dst, sems.at[i])
        for i, (src, dst) in enumerate(((len_hbm, lens), (own_hbm, owns), (x_hbm, x_ref), (c_hbm, c_ref)))
    ]
    for copy in copies:
        copy.start()
    users = lens.shape[0]
    owners = users // 2
    last = x_ref.shape[1] - LANES
    for j in range(owners):
        seen[j] = 0
    copies[0].wait()
    copies[1].wait()

    def user(u, off):
        own = owns[u]
        length = lens[u]
        second = seen[own]
        seen[own] = 1
        start = second * (LANES - length)
        table[u] = off
        table[users + u] = start
        table[2 * users + u] = length
        table[3 * users + u] = own
        tab[second, own] = off - start
        tab[2 + second, own] = length
        return off + length

    lax.fori_loop(0, users, user, 0, unroll=16)
    mine = tab[2, me_ref[0]]

    def fill(i, carry):
        table[4 * users + i] = mine
        return carry

    lax.fori_loop(0, users, fill, 0, unroll=16)
    copies[2].wait()
    copies[3].wait()
    lane = lax.broadcasted_iota(jnp.int32, (16, LANES), 1)

    def owner(j, carry):
        both = []
        for k in range(2):
            first = tab[k, j]
            inside = first & (LANES - 1)
            base = pl.multiple_of(first - inside, LANES)
            after = pl.multiple_of(jnp.minimum(base + LANES, last), LANES)
            back = (LANES - inside) & (LANES - 1)
            low = lane >= inside
            both.append(
                [
                    pltpu.roll(jnp.where(low, ref[:, pl.ds(base, LANES)], ref[:, pl.ds(after, LANES)]), back, 1)
                    for ref in (x_ref, c_ref)
                ]
            )
        head = lane < tab[2, j]
        out_ref[j, 0:16, :] = jnp.where(head, both[0][0], both[1][0])
        out_ref[j, 16:32, :] = jnp.where(head, both[0][1], both[1][1])
        return carry

    lax.fori_loop(0, owners, owner, 0, unroll=8)


def unpack_kernel(table, got_ref, out_ref, wide):
    users = table.shape[0] // 5
    lane = lax.broadcasted_iota(jnp.int32, (16, LANES), 1)

    def user(u, carry):
        off = table[u]
        inside = off & (LANES - 1)
        base = pl.multiple_of(off - inside, LANES)
        turn = (inside - table[users + u]) & (LANES - 1)
        moved = pltpu.roll(got_ref[table[3 * users + u], 0:16, :], turn, 1).astype(F32)
        end = inside + table[2 * users + u]
        pltpu.store(wide.at[:, pl.ds(base, LANES)], moved, mask=(lane >= inside) & (lane < end))
        pltpu.store(wide.at[:, pl.ds(base + LANES, LANES)], moved, mask=lane < end - LANES)
        return carry

    lax.fori_loop(0, users, user, 0, unroll=16)
    out_ref[...] = wide[:, : out_ref.shape[1]].astype(BF)


def sigmoid(v):
    return 0.5 * jnp.tanh(0.5 * v) + 0.5


def norm_parts(v):
    center = v - jnp.mean(v, axis=-1, keepdims=True)
    rstd = lax.rsqrt(jnp.mean(center * center, axis=-1, keepdims=True) + EPS)
    return center * rstd, rstd


def norm_back(hat, rstd, d):
    return rstd * (d - jnp.mean(d, axis=-1, keepdims=True) - hat * jnp.mean(d * hat, axis=-1, keepdims=True))


def forward_kernel(pos_ref, table, rc_ref, w_in_hbm, acts_ref, slope_ref, wts_ref, wslope_ref, ahat_ref, arstd_ref, swap_ref, w_in, sems):
    width = rc_ref.shape[0] * 16
    rows = rc_ref.shape[2]
    per = w_in.shape[1] // WEIGHT_CHUNKS

    def fetch(i):
        part = pl.ds(i * per, per)
        return pltpu.make_async_copy(w_in_hbm.at[:, part], w_in.at[:, part], sems.at[i])

    order = [2, 3, 4, 5, 6, 7, 0, 1]
    for i in order:
        fetch(i).start()
    x = rc_ref[:, 0:16, :].reshape(width, rows).T
    normed = norm_parts(x.astype(F32))[0].astype(BF)
    for i in order:
        fetch(i).wait()
        part = slice(i * per, (i + 1) * per)
        pre = dot(normed, w_in[:, part], 1, 0)
        gate = sigmoid(pre)
        act = pre * gate
        acts_ref[:, part] = act.astype(BF)
        slope_ref[:, part] = (gate + act * (1.0 - gate)).astype(BF)
    query = lax.broadcasted_iota(jnp.int32, (rows, rows), 0)
    key = lax.broadcasted_iota(jnp.int32, (rows, rows), 1)
    first = table[table.shape[0] - 1]
    allowed = ((query < first) == (key < first)) & (key <= query)
    each = width // HEADS
    scale = float(each) ** -0.5
    attended = []
    for h in range(HEADS):
        v = acts_ref[:, width + h * each : width + (h + 1) * each]
        q = acts_ref[:, 2 * width + h * each : 2 * width + (h + 1) * each]
        k = acts_ref[:, 3 * width + h * each : 3 * width + (h + 1) * each]
        scores = dot(q, k, 1, 1) * scale
        gate = sigmoid(scores)
        weight = scores * gate
        kept = jnp.where(allowed, weight, 0.0).astype(BF)
        wts_ref[h] = kept
        wslope_ref[h] = jnp.where(allowed, (gate + weight * (1.0 - gate)) * scale, 0.0).astype(BF)
        attended.append(dot(kept, v, 1, 0))
    hat, rstd = norm_parts(jnp.concatenate(attended, axis=1))
    ahat_ref[...] = hat
    arstd_ref[...] = jnp.broadcast_to(rstd, arstd_ref.shape)
    swap_ref[:width] = (hat * acts_ref[:, :width].astype(F32)).astype(BF).T
    for y in range(4):
        block = y * 2 + 1 - pos_ref[0]
        swap_ref[width + y * LANES : width + (y + 1) * LANES] = rc_ref[pl.ds(block * 8, 8), 16:32, :].reshape(LANES, rows)


def mixed_grad_kernel(rc_ref, w_out_ref, d_mixed_ref):
    cots = rc_ref[:, 16:32, :].reshape(-1, LANES)
    d_mixed_ref[...] = dot(cots, w_out_ref[...], 0, 1).astype(BF)


def product_kernel(pos_ref, rc_ref, own_ref, got_ref, order_hbm, *out_refs):
    width = rc_ref.shape[0] * 16
    core, y = pos_ref[0], pos_ref[1]
    left, right = [], []
    for k in range(4):
        to = (y + k) & 3
        left.append(rc_ref[pl.ds((to * 2 + core) * 8, 8), 16:32, :].reshape(LANES, LANES))
        right.append(got_ref[pl.ds(pl.multiple_of(width + to * LANES, LANES), LANES), :])
    cots = jnp.concatenate([jnp.concatenate(left, axis=0), jnp.concatenate(right, axis=0)], axis=1)
    step = 256
    for i in range(width // step):
        part = slice(i * step, (i + 1) * step)
        mixed = jnp.concatenate([own_ref[part], got_ref[part]], axis=1)
        term = dot(mixed, cots, 1, 1).astype(BF)
        for k in range(4):
            out_refs[k][part] = term[:, k * LANES : (k + 1) * LANES]


def backward_kernel(rc_ref, d_mixed_ref, acts_ref, slope_ref, wts_ref, wslope_ref, ahat_ref, arstd_ref, w_in_hbm, grad_ref, w_in, d_pre, sems):
    width = rc_ref.shape[0] * 16
    rows = rc_ref.shape[2]
    per = w_in.shape[1] // WEIGHT_CHUNKS

    def fetch(i):
        part = pl.ds(i * per, per)
        return pltpu.make_async_copy(w_in_hbm.at[:, part], w_in.at[:, part], sems.at[i])

    for i in range(WEIGHT_CHUNKS):
        fetch(i).start()
    cots = rc_ref[:, 16:32, :].reshape(width, rows).T
    d_mixed = d_mixed_ref[...].astype(F32)
    hat = ahat_ref[...]
    d_pre[:, :width] = ((d_mixed * hat) * slope_ref[:, :width].astype(F32)).astype(BF)
    d_att = norm_back(hat, arstd_ref[:, 0:1], d_mixed * acts_ref[:, :width].astype(F32)).astype(BF)
    each = width // HEADS
    for h in range(HEADS):
        vs = slice(width + h * each, width + (h + 1) * each)
        qs = slice(2 * width + h * each, 2 * width + (h + 1) * each)
        ks = slice(3 * width + h * each, 3 * width + (h + 1) * each)
        da = d_att[:, h * each : (h + 1) * each]
        d_weight = dot(da, acts_ref[:, vs], 1, 1)
        d_score = (d_weight * wslope_ref[h].astype(F32)).astype(BF)
        d_pre[:, vs] = (dot(wts_ref[h], da, 0, 0) * slope_ref[:, vs].astype(F32)).astype(BF)
        d_pre[:, qs] = (dot(d_score, acts_ref[:, ks], 1, 0) * slope_ref[:, qs].astype(F32)).astype(BF)
        d_pre[:, ks] = (dot(d_score, acts_ref[:, qs], 0, 0) * slope_ref[:, ks].astype(F32)).astype(BF)
    d_normed = jnp.zeros((rows, width), F32)
    for i in range(WEIGHT_CHUNKS):
        fetch(i).wait()
        part = slice(i * per, (i + 1) * per)
        d_normed += dot(d_pre[:, part], w_in[:, part], 1, 1)
    x = rc_ref[:, 0:16, :].reshape(width, rows).T
    normed, rstd = norm_parts(x.astype(F32))
    grad = norm_back(normed, rstd, d_normed) + cots.astype(F32)
    grad_ref[...] = grad.astype(BF).T.reshape(grad_ref.shape)


def merge_kernel(grad_ref, *refs):
    total = refs[0][...].astype(F32)
    for part in refs[1:-1]:
        total += part[...].astype(F32)
    out_ref = refs[-1]
    out_ref[:, 0:16, :] = grad_ref[...]
    out_ref[:, 16:32, :] = total.astype(BF).reshape(grad_ref.shape)


def last_sum_kernel(got_ref, out_ref):
    for side in range(2):
        total = got_ref[side, 16:32, :].astype(F32)
        for i in range(side + 2, got_ref.shape[0], 2):
            total += got_ref[i, 16:32, :].astype(F32)
        out_ref[:, side * LANES : (side + 1) * LANES] = total


def join_kernel(pos_ref, *refs):
    y = pos_ref[1]
    for k in range(4):
        at = (y + 4 - k) & 3
        refs[-1][:, pl.ds(pl.multiple_of(at * 256, 256), 256)] = refs[k][...]


def further(k):
    return [(i, (i + k) % 4) for i in range(4)]


def per_device(looked, cotangent, w_in, w_out, lengths, owner):
    cols = lax.axis_size("col")
    events, mine_cols = looked.shape
    width = w_out.shape[0]
    rows = events // cols
    users = lengths.shape[0]
    me = lax.axis_index("col")
    pos = jnp.stack([me % 2, lax.axis_index("rep"), me // 2 % 4, me // 8]).astype(jnp.int32)
    send, table = pl.pallas_call(
        pack_kernel,
        out_shape=(shape((cols, 2 * mine_cols, rows)), shape((5 * users,), jnp.int32)),
        in_specs=[ANY, ANY, SMEM, ANY, ANY],
        out_specs=(VMEM, SMEM),
        scratch_shapes=[
            pltpu.SMEM((users,), jnp.int32),
            pltpu.SMEM((users,), jnp.int32),
            pltpu.VMEM((mine_cols, events), BF),
            pltpu.VMEM((mine_cols, events), BF),
            pltpu.SMEM((4, cols), jnp.int32),
            pltpu.SMEM((cols,), jnp.int32),
            pltpu.SemaphoreType.DMA((4,)),
        ],
        compiler_params=params(60),
    )(lengths, owner, me.reshape(1).astype(jnp.int32), looked.T, cotangent.T)
    packed = lax.all_to_all(send, "col", split_axis=0, concat_axis=0, tiled=True)
    acts, slope, wts, wslope, ahat, arstd, swap = pl.pallas_call(
        forward_kernel,
        out_shape=(
            shape((rows, 4 * width)),
            shape((rows, 4 * width)),
            shape((HEADS, rows, rows)),
            shape((HEADS, rows, rows)),
            shape((rows, width), F32),
            shape((rows, LANES), F32),
            shape((width + width // 2, rows)),
        ),
        in_specs=[SMEM, SMEM, VMEM, ANY],
        scratch_shapes=[pltpu.VMEM(w_in.shape, BF), pltpu.SemaphoreType.DMA((WEIGHT_CHUNKS,))],
        compiler_params=params(48),
    )(pos, table, packed, w_in)
    got = lax.ppermute(swap, "col", [(i, i ^ 1) for i in range(cols)])
    d_mixed = pl.pallas_call(mixed_grad_kernel, out_shape=shape((rows, width)), compiler_params=params(32))(packed, w_out)
    terms = pl.pallas_call(
        product_kernel,
        out_shape=[shape((width, LANES))] * 4,
        in_specs=[SMEM, VMEM, VMEM, VMEM, ANY],
        compiler_params=params(32),
    )(pos, packed, swap, got, d_mixed)
    terms = [terms[0]] + [lax.ppermute(terms[k], "rep", further(k)) for k in range(1, 4)]
    grad = pl.pallas_call(
        backward_kernel,
        out_shape=shape((cols, mine_cols, rows)),
        in_specs=[VMEM] * 8 + [ANY],
        scratch_shapes=[
            pltpu.VMEM(w_in.shape, BF),
            pltpu.VMEM((rows, 4 * width), BF),
            pltpu.SemaphoreType.DMA((WEIGHT_CHUNKS,)),
        ],
        compiler_params=params(48),
    )(packed, d_mixed, acts, slope, wts, wslope, ahat, arstd, w_in)
    merged = pl.pallas_call(merge_kernel, out_shape=shape((cols, 2 * mine_cols, rows)), compiler_params=params(32))(grad, *terms)
    back = lax.all_to_all(merged, "col", split_axis=0, concat_axis=0, tiled=True)
    mine = pl.pallas_call(last_sum_kernel, out_shape=shape((mine_cols, 2 * LANES), F32), compiler_params=params(32))(back)
    parts = [mine] + [lax.ppermute(mine, "rep", further(k)) for k in range(1, 4)]
    d_looked = pl.pallas_call(
        unpack_kernel,
        out_shape=shape((mine_cols, events)),
        in_specs=[SMEM, VMEM],
        scratch_shapes=[pltpu.VMEM((mine_cols, events + LANES), F32)],
        compiler_params=params(32),
    )(table, back)
    d_w_out = pl.pallas_call(
        join_kernel, out_shape=shape((mine_cols, width), F32), in_specs=[SMEM] + [VMEM] * 4, compiler_params=params(32)
    )(pos, *parts)
    return (d_looked.T, d_w_out)


def solution(mesh):
    placed = (P("rep", "col"), P("rep", "col"), P(), P(), P("rep"), P("rep"))
    return jax.shard_map(
        per_device,
        mesh=mesh,
        in_specs=placed,
        out_specs=(P("rep", "col"), P("col", None)),
        check_vma=False,
    )
```

```python
import functools

import jax
import jax.numpy as jnp
from jax import lax
from jax.experimental import pallas as pl
from jax.experimental.pallas import tpu as pltpu
from jax.sharding import PartitionSpec as P

HEADS = 8
EPS = 1e-05
BF = jnp.bfloat16
F32 = jnp.float32
LANES = 128
CHUNKS = 8
IN_FLIGHT = 8
HALVES = ((0, 1, 2, 4, 6), (3, 5, 7))
USERS_AT_ONCE = 32
OWNERS_AT_ONCE = 8
MOVES_AT_ONCE = 16

SMEM = pl.BlockSpec(memory_space=pltpu.SMEM)
VMEM = pl.BlockSpec(memory_space=pltpu.VMEM)
ANY = pl.BlockSpec(memory_space=pl.ANY)
HBM = pl.BlockSpec(memory_space=pltpu.HBM)


def params(mib):
    return pltpu.CompilerParams(vmem_limit_bytes=mib << 20)


def core_index():
    return lax.axis_index("col") & 1


def shape(dims, dtype=BF):
    return jax.ShapeDtypeStruct(dims, dtype)


def dot(a, b, ca, cb):
    return lax.dot_general(a, b, (((ca,), (cb,)), ((), ())), preferred_element_type=F32)


def pack_kernel(len_hbm, own_hbm, x_hbm, c_hbm, out_ref, table, mine_ref, x_ref, c_ref, tab, seen, sems):
    users = len_hbm.shape[0]
    lens, owns = table.at[pl.ds(2 * users, users)], table.at[pl.ds(3 * users, users)]
    copies = [
        pltpu.make_async_copy(src, dst, sems.at[i])
        for i, (src, dst) in enumerate(((len_hbm, lens), (own_hbm, owns), (x_hbm, x_ref), (c_hbm, c_ref)))
    ]
    for copy in copies:
        copy.start()
    owners = users // 2
    last = x_ref.shape[1] - LANES
    for j in range(owners):
        seen[j] = 0
    copies[0].wait()
    copies[1].wait()

    def user(u, off):
        own = table[3 * users + u]
        length = table[2 * users + u]
        second = seen[own]
        seen[own] = 1
        start = second * (LANES - length)
        table[u] = off
        table[users + u] = start
        tab[second, own] = off - start
        tab[2 + second, own] = length
        return off + length

    lax.fori_loop(0, users, user, 0, unroll=USERS_AT_ONCE)
    mine_ref[...] = jnp.full(mine_ref.shape, tab[2, lax.axis_index("col")], jnp.int32)
    copies[2].wait()
    copies[3].wait()
    lane = lax.broadcasted_iota(jnp.int32, (16, LANES), 1)

    def owner(j, carry):
        both = []
        for k in range(2):
            first = tab[k, j]
            inside = first & (LANES - 1)
            base = pl.multiple_of(first - inside, LANES)
            after = pl.multiple_of(jnp.minimum(base + LANES, last), LANES)
            back = (LANES - inside) & (LANES - 1)
            low = lane >= inside
            both.append(
                [
                    pltpu.roll(jnp.where(low, ref[:, pl.ds(base, LANES)], ref[:, pl.ds(after, LANES)]), back, 1)
                    for ref in (x_ref, c_ref)
                ]
            )
        head = lane < tab[2, j]
        out_ref[j, 0:16, :] = jnp.where(head, both[0][0], both[1][0])
        out_ref[j, 16:32, :] = jnp.where(head, both[0][1], both[1][1])
        return carry

    lax.fori_loop(0, owners, owner, 0, unroll=OWNERS_AT_ONCE)


def unpack_kernel(table, got_ref, out_ref, wide):
    users = table.shape[0] // 4
    lane = lax.broadcasted_iota(jnp.int32, (16, LANES), 1)

    def user(u, carry):
        off = table[u]
        own = table[3 * users + u]
        inside = off & (LANES - 1)
        base = pl.multiple_of(off - inside, LANES)
        turn = (inside - table[users + u]) & (LANES - 1)
        moved = pltpu.roll(got_ref[own >> 1, pl.ds(pl.multiple_of((own & 1) * 16, 16), 16), :], turn, 1).astype(F32)
        end = inside + table[2 * users + u]
        pltpu.store(wide.at[:, pl.ds(base, LANES)], moved, mask=(lane >= inside) & (lane < end))
        pltpu.store(wide.at[:, pl.ds(base + LANES, LANES)], moved, mask=lane < end - LANES)
        return carry

    lax.fori_loop(0, users, user, 0, unroll=MOVES_AT_ONCE)
    out_ref[...] = wide[:, : out_ref.shape[1]].astype(BF)


def sigmoid(v):
    return 0.5 * jnp.tanh(0.5 * v) + 0.5


def norm_parts(v):
    center = v - jnp.mean(v, axis=-1, keepdims=True)
    rstd = lax.rsqrt(jnp.mean(center * center, axis=-1, keepdims=True) + EPS)
    return center * rstd, rstd


def norm_back(hat, rstd, d):
    return rstd * (d - jnp.mean(d, axis=-1, keepdims=True) - hat * jnp.mean(d * hat, axis=-1, keepdims=True))


def column_chunks(w_hbm, w_ref, sems, order):
    per = w_hbm.shape[1] // len(order)

    def copy(i):
        part = pl.ds(order[i] * per, per)
        return pltpu.make_async_copy(w_hbm.at[:, part], w_ref.at[:, part], sems.at[i])

    def start(i):
        if i < len(order):
            copy(i).start()

    def wait(i):
        copy(i).wait()
        start(i + IN_FLIGHT)
        return slice(order[i] * per, (order[i] + 1) * per)

    for i in range(IN_FLIGHT):
        start(i)
    return wait


def forward_kernel(mine_ref, rc_ref, w_hbm, acts_ref, slope_ref, wts_ref, wslope_ref, ahat_ref, arstd_ref, keep_ref, swap_ref, w_in, sems):
    width = rc_ref.shape[0] * 16
    rows = rc_ref.shape[2]
    order = HALVES[0] + HALVES[1]
    wait = column_chunks(w_hbm, w_in, sems, order)
    x = rc_ref[:, 0:16, :].reshape(width, rows).T
    normed = norm_parts(x.astype(F32))[0].astype(BF)
    query = lax.broadcasted_iota(jnp.int32, (rows, rows), 0)
    key = lax.broadcasted_iota(jnp.int32, (rows, rows), 1)
    first = mine_ref[0:1, :]
    allowed = ((query < first) == (key < first)) & (key <= query)
    each = width // HEADS
    scale = float(each) ** -0.5
    attended = []
    for half in range(2):
        for i in range(len(HALVES[half])):
            part = wait(i + half * len(HALVES[0]))
            pre = dot(normed, w_in[:, part], 1, 0)
            gate = sigmoid(pre)
            act = pre * gate
            acts_ref[:, part] = act.astype(BF)
            slope_ref[:, part] = (gate + act * (1.0 - gate)).astype(BF)
        for h in range(half * HEADS // 2, (half + 1) * HEADS // 2):
            v = acts_ref[:, width + h * each : width + (h + 1) * each]
            q = acts_ref[:, 2 * width + h * each : 2 * width + (h + 1) * each]
            k = acts_ref[:, 3 * width + h * each : 3 * width + (h + 1) * each]
            scores = dot(q, k, 1, 1) * scale
            gate = sigmoid(scores)
            weight = scores * gate
            kept = jnp.where(allowed, weight, 0.0).astype(BF)
            wts_ref[h] = kept
            wslope_ref[h] = jnp.where(allowed, (gate + weight * (1.0 - gate)) * scale, 0.0).astype(BF)
            attended.append(dot(kept, v, 1, 0))
    hat, rstd = norm_parts(jnp.concatenate(attended, axis=1))
    ahat_ref[...] = hat
    arstd_ref[...] = jnp.broadcast_to(rstd, arstd_ref.shape)
    mixed = (hat * acts_ref[:, :width].astype(F32)).astype(BF).T.reshape(32, 2, 16, rows)
    even = core_index() == 0
    keep_ref[...] = jnp.where(even, mixed[:, 0], mixed[:, 1]).reshape(width // 2, rows)
    swap_ref[: width // 2] = jnp.where(even, mixed[:, 1], mixed[:, 0]).reshape(width // 2, rows)
    swap_ref[width // 2 :] = rc_ref[:, 16:32, :].reshape(width, rows)


def mixed_grad_kernel(rc_ref, w_out_ref, d_mixed_ref):
    cots = rc_ref[:, 16:32, :].reshape(-1, LANES)
    d_mixed_ref[...] = dot(cots, w_out_ref[...], 0, 1).astype(BF)


def product_kernel(rc_ref, own_ref, got_ref, order_hbm, *out_refs):
    half = own_ref.shape[0]
    mixed = jnp.concatenate([own_ref[...], got_ref[:half]], axis=1)
    for k, out in enumerate(out_refs):
        to = (lax.axis_index("rep") + k) & 3
        left = rc_ref[pl.ds(to * 16, 16), 16:32, :].reshape(256, LANES)
        right = got_ref[pl.ds(pl.multiple_of(half + to * 256, 256), 256), :]
        term = dot(mixed, jnp.concatenate([left, right], axis=1), 1, 1).astype(BF)
        out[:, 0:16, :] = term[:, :LANES].reshape(32, 16, LANES)
        out[:, 16:32, :] = term[:, LANES:].reshape(32, 16, LANES)


def backward_kernel(rc_ref, d_mixed_ref, acts_ref, slope_ref, wts_ref, wslope_ref, ahat_ref, arstd_ref, w_hbm, keep_ref, swap_ref, w_in, d_pre, sems):
    width = rc_ref.shape[0] * 16
    rows = rc_ref.shape[2]
    wait = column_chunks(w_hbm, w_in, sems, list(range(CHUNKS)))
    d_mixed = d_mixed_ref[...].astype(F32)
    hat = ahat_ref[...]
    d_pre[:, :width] = ((d_mixed * hat) * slope_ref[:, :width].astype(F32)).astype(BF)
    d_att = norm_back(hat, arstd_ref[:, 0:1], d_mixed * acts_ref[:, :width].astype(F32)).astype(BF)
    each = width // HEADS
    for h in range(HEADS):
        vs = slice(width + h * each, width + (h + 1) * each)
        qs = slice(2 * width + h * each, 2 * width + (h + 1) * each)
        ks = slice(3 * width + h * each, 3 * width + (h + 1) * each)
        da = d_att[:, h * each : (h + 1) * each]
        d_weight = dot(da, acts_ref[:, vs], 1, 1)
        d_score = (d_weight * wslope_ref[h].astype(F32)).astype(BF)
        d_pre[:, vs] = (dot(wts_ref[h], da, 0, 0) * slope_ref[:, vs].astype(F32)).astype(BF)
        d_pre[:, qs] = (dot(d_score, acts_ref[:, ks], 1, 0) * slope_ref[:, qs].astype(F32)).astype(BF)
        d_pre[:, ks] = (dot(d_score, acts_ref[:, qs], 0, 0) * slope_ref[:, ks].astype(F32)).astype(BF)
    d_normed = jnp.zeros((rows, width), F32)
    for i in range(CHUNKS):
        part = wait(i)
        d_normed += dot(d_pre[:, part], w_in[:, part], 1, 1)
    cots = rc_ref[:, 16:32, :].reshape(width, rows).T
    x = rc_ref[:, 0:16, :].reshape(width, rows).T
    normed, rstd = norm_parts(x.astype(F32))
    grad = norm_back(normed, rstd, d_normed) + cots.astype(F32)
    grad = grad.astype(BF).T.reshape(32, 2, 16, rows)
    even = core_index() == 0
    keep_ref[...] = jnp.where(even, grad[:, 0], grad[:, 1])
    swap_ref[...] = jnp.where(even, grad[:, 1], grad[:, 0])


def merge_kernel(keep_ref, swapped_ref, *refs):
    out_ref = refs[-1]
    core = core_index()
    out_ref[:, pl.ds(pl.multiple_of(core * 16, 16), 16), :] = keep_ref[...]
    out_ref[:, pl.ds(pl.multiple_of((1 - core) * 16, 16), 16), :] = swapped_ref[...]
    total = refs[0][...].astype(F32)
    for part in refs[1:-1]:
        total += part[...].astype(F32)
    out_ref[:, 32:64, :] = total.astype(BF)


def last_sum_kernel(got_ref, out_ref):
    total = got_ref[0, 32:64, :].astype(F32)
    for i in range(1, got_ref.shape[0]):
        total += got_ref[i, 32:64, :].astype(F32)
    out_ref[:, :LANES] = total[0:16]
    out_ref[:, LANES:] = total[16:32]


def join_kernel(*refs):
    y = lax.axis_index("rep")
    for k in range(4):
        at = (y + 4 - k) & 3
        refs[-1][:, pl.ds(pl.multiple_of(at * 256, 256), 256)] = refs[k][...]


def further(k):
    return [(i, (i + k) % 4) for i in range(4)]


def per_device(looked, cotangent, w_in, w_out, lengths, owner):
    cols = lax.axis_size("col")
    events, mine_cols = looked.shape
    width = w_out.shape[0]
    rows = events // cols
    users = lengths.shape[0]
    send, table, first = pl.pallas_call(
        pack_kernel,
        out_shape=(
            shape((cols, 2 * mine_cols, rows)),
            shape((4 * users,), jnp.int32),
            shape((8, LANES), jnp.int32),
        ),
        in_specs=[HBM] * 4,
        out_specs=(VMEM, SMEM, VMEM),
        scratch_shapes=[
            pltpu.VMEM((mine_cols, events), BF),
            pltpu.VMEM((mine_cols, events), BF),
            pltpu.SMEM((4, cols), jnp.int32),
            pltpu.SMEM((cols,), jnp.int32),
            pltpu.SemaphoreType.DMA((4,)),
        ],
        compiler_params=params(60),
    )(lengths, owner, looked.T, cotangent.T)
    packed = lax.all_to_all(send, "col", split_axis=0, concat_axis=0, tiled=True)
    acts, slope, wts, wslope, ahat, arstd, keep, swap = pl.pallas_call(
        forward_kernel,
        out_shape=(
            shape((rows, 4 * width)),
            shape((rows, 4 * width)),
            shape((HEADS, rows, rows)),
            shape((HEADS, rows, rows)),
            shape((rows, width), F32),
            shape((rows, LANES), F32),
            shape((width // 2, rows)),
            shape((width + width // 2, rows)),
        ),
        in_specs=[VMEM, VMEM, HBM],
        scratch_shapes=[pltpu.VMEM(w_in.shape, BF), pltpu.SemaphoreType.DMA((CHUNKS,))],
        compiler_params=params(48),
    )(first, packed, w_in)
    other_core = [(i, i ^ 1) for i in range(cols)]
    got = lax.ppermute(swap, "col", other_core)
    d_mixed = pl.pallas_call(mixed_grad_kernel, out_shape=shape((rows, width)), compiler_params=params(16))(packed, w_out)
    block = (cols // 2, 2 * mine_cols, LANES)
    terms = pl.pallas_call(
        product_kernel,
        out_shape=[shape(block)] * 4,
        in_specs=[VMEM, VMEM, VMEM, ANY],
        compiler_params=params(16),
    )(packed, keep, got, d_mixed)
    terms = [terms[0]] + [lax.ppermute(terms[k], "rep", further(k)) for k in range(1, 4)]
    grad, swap = pl.pallas_call(
        backward_kernel,
        out_shape=[shape((cols // 2, mine_cols, rows))] * 2,
        in_specs=[VMEM] * 8 + [HBM],
        scratch_shapes=[
            pltpu.VMEM(w_in.shape, BF),
            pltpu.VMEM((rows, 4 * width), BF),
            pltpu.SemaphoreType.DMA((CHUNKS,)),
        ],
        compiler_params=params(48),
    )(packed, d_mixed, acts, slope, wts, wslope, ahat, arstd, w_in)
    swapped = lax.ppermute(swap, "col", other_core)
    merged = pl.pallas_call(
        merge_kernel,
        out_shape=shape((cols // 2, 4 * mine_cols, rows)),
        in_specs=[VMEM] * 6,
        compiler_params=params(16),
    )(grad, swapped, *terms)
    same_core = [list(range(core, cols, 2)) for core in range(2)]
    back = lax.all_to_all(merged, "col", split_axis=0, concat_axis=0, axis_index_groups=same_core, tiled=True)
    mine = pl.pallas_call(last_sum_kernel, out_shape=shape((mine_cols, 2 * LANES), F32), compiler_params=params(16))(back)
    parts = [mine] + [lax.ppermute(mine, "rep", further(k)) for k in range(1, 4)]
    d_looked = pl.pallas_call(
        unpack_kernel,
        out_shape=shape((mine_cols, events)),
        in_specs=[SMEM, VMEM],
        scratch_shapes=[pltpu.VMEM((mine_cols, events + LANES), F32)],
        compiler_params=params(16),
    )(table, back)
    d_w_out = pl.pallas_call(
        join_kernel, out_shape=shape((mine_cols, width), F32), in_specs=[VMEM] * 4, compiler_params=params(16)
    )(*parts)
    return (d_looked.T, d_w_out)


def solution(mesh):
    placed = (P("rep", "col"), P("rep", "col"), P(), P(), P("rep"), P("rep"))
    return jax.shard_map(
        per_device,
        mesh=mesh,
        in_specs=placed,
        out_specs=(P("rep", "col"), P("col", None)),
        check_vma=False,
    )
```

```python
import functools

import jax
import jax.numpy as jnp
from jax import lax
from jax.experimental import pallas as pl
from jax.experimental.pallas import tpu as pltpu
from jax.sharding import PartitionSpec as P

HEADS = 8
EPS = 1e-05
BF = jnp.bfloat16
F32 = jnp.float32
LANES = 128
CHUNKS = 8
IN_FLIGHT = 8
HALVES = ((0, 1, 2, 4, 6), (3, 5, 7))
USERS_AT_ONCE = 32
OWNERS_AT_ONCE = 8
MOVES_AT_ONCE = 16

SMEM = pl.BlockSpec(memory_space=pltpu.SMEM)
VMEM = pl.BlockSpec(memory_space=pltpu.VMEM)
ANY = pl.BlockSpec(memory_space=pl.ANY)
HBM = pl.BlockSpec(memory_space=pltpu.HBM)


def params(mib):
    return pltpu.CompilerParams(vmem_limit_bytes=mib << 20)


def core_index():
    return lax.axis_index("col") & 1


def shape(dims, dtype=BF):
    return jax.ShapeDtypeStruct(dims, dtype)


def dot(a, b, ca, cb):
    return lax.dot_general(a, b, (((ca,), (cb,)), ((), ())), preferred_element_type=F32)


def pack_kernel(len_hbm, own_hbm, x_hbm, c_hbm, out_ref, table, mine_hbm, x_ref, c_ref, tab, seen, mine, sems):
    users = len_hbm.shape[0]
    lens, owns = table.at[pl.ds(2 * users, users)], table.at[pl.ds(3 * users, users)]
    copies = [
        pltpu.make_async_copy(src, dst, sems.at[i])
        for i, (src, dst) in enumerate(((len_hbm, lens), (own_hbm, owns), (x_hbm, x_ref), (c_hbm, c_ref)))
    ]
    for copy in copies:
        copy.start()
    owners = users // 2
    last = x_ref.shape[1] - LANES
    for j in range(owners):
        seen[j] = 0
    copies[0].wait()
    copies[1].wait()

    def user(u, off):
        own = table[3 * users + u]
        length = table[2 * users + u]
        second = seen[own]
        seen[own] = 1
        start = second * (LANES - length)
        table[u] = off
        table[users + u] = start
        tab[second, own] = off - start
        tab[2 + second, own] = length
        return off + length

    lax.fori_loop(0, users, user, 0, unroll=USERS_AT_ONCE)
    mine[...] = jnp.full(mine.shape, tab[2, lax.axis_index("col")], jnp.int32)
    tell = pltpu.make_async_copy(mine, mine_hbm.at[pl.ds(0, mine.shape[0])], sems.at[4])
    tell.start()
    copies[2].wait()
    copies[3].wait()
    lane = lax.broadcasted_iota(jnp.int32, (16, LANES), 1)

    def owner(j, carry):
        both = []
        for k in range(2):
            first = tab[k, j]
            inside = first & (LANES - 1)
            base = pl.multiple_of(first - inside, LANES)
            after = pl.multiple_of(jnp.minimum(base + LANES, last), LANES)
            back = (LANES - inside) & (LANES - 1)
            low = lane >= inside
            both.append(
                [
                    pltpu.roll(jnp.where(low, ref[:, pl.ds(base, LANES)], ref[:, pl.ds(after, LANES)]), back, 1)
                    for ref in (x_ref, c_ref)
                ]
            )
        head = lane < tab[2, j]
        out_ref[j, 0:16, :] = jnp.where(head, both[0][0], both[1][0])
        out_ref[j, 16:32, :] = jnp.where(head, both[0][1], both[1][1])
        return carry

    lax.fori_loop(0, owners, owner, 0, unroll=OWNERS_AT_ONCE)
    tell.wait()


def unpack_kernel(table, got_ref, out_ref, wide):
    users = table.shape[0] // 4
    lane = lax.broadcasted_iota(jnp.int32, (16, LANES), 1)

    def user(u, carry):
        off = table[u]
        own = table[3 * users + u]
        inside = off & (LANES - 1)
        base = pl.multiple_of(off - inside, LANES)
        turn = (inside - table[users + u]) & (LANES - 1)
        moved = pltpu.roll(got_ref[own >> 1, pl.ds(pl.multiple_of((own & 1) * 16, 16), 16), :], turn, 1).astype(F32)
        end = inside + table[2 * users + u]
        pltpu.store(wide.at[:, pl.ds(base, LANES)], moved, mask=(lane >= inside) & (lane < end))
        pltpu.store(wide.at[:, pl.ds(base + LANES, LANES)], moved, mask=lane < end - LANES)
        return carry

    lax.fori_loop(0, users, user, 0, unroll=MOVES_AT_ONCE)
    out_ref[...] = wide[:, : out_ref.shape[1]].astype(BF)


def sigmoid(v):
    return 0.5 * jnp.tanh(0.5 * v) + 0.5


def norm_parts(v):
    center = v - jnp.mean(v, axis=-1, keepdims=True)
    rstd = lax.rsqrt(jnp.mean(center * center, axis=-1, keepdims=True) + EPS)
    return center * rstd, rstd


def norm_back(hat, rstd, d):
    return rstd * (d - jnp.mean(d, axis=-1, keepdims=True) - hat * jnp.mean(d * hat, axis=-1, keepdims=True))


def column_chunks(w_hbm, w_ref, sems, order):
    per = w_hbm.shape[1] // len(order)

    def copy(i):
        part = pl.ds(order[i] * per, per)
        return pltpu.make_async_copy(w_hbm.at[:, part], w_ref.at[:, part], sems.at[i])

    def start(i):
        if i < len(order):
            copy(i).start()

    def wait(i):
        copy(i).wait()
        start(i + IN_FLIGHT)
        return slice(order[i] * per, (order[i] + 1) * per)

    for i in range(IN_FLIGHT):
        start(i)
    return wait


def forward_kernel(mine_hbm, rc_ref, w_hbm, acts_ref, slope_ref, wts_ref, wslope_ref, ahat_ref, arstd_ref, keep_ref, swap_ref, w_in, mine, sems):
    width = rc_ref.shape[0] * 16
    rows = rc_ref.shape[2]
    tell = pltpu.make_async_copy(mine_hbm.at[pl.ds(0, mine.shape[0])], mine, sems.at[CHUNKS])
    tell.start()
    order = HALVES[0] + HALVES[1]
    wait = column_chunks(w_hbm, w_in, sems, order)
    x = rc_ref[:, 0:16, :].reshape(width, rows).T
    normed = norm_parts(x.astype(F32))[0].astype(BF)
    query = lax.broadcasted_iota(jnp.int32, (rows, rows), 0)
    key = lax.broadcasted_iota(jnp.int32, (rows, rows), 1)
    tell.wait()
    first = mine[0:1, :]
    allowed = ((query < first) == (key < first)) & (key <= query)
    each = width // HEADS
    scale = float(each) ** -0.5
    attended = []
    for half in range(2):
        for i in range(len(HALVES[half])):
            part = wait(i + half * len(HALVES[0]))
            pre = dot(normed, w_in[:, part], 1, 0)
            gate = sigmoid(pre)
            act = pre * gate
            acts_ref[:, part] = act.astype(BF)
            slope_ref[:, part] = (gate + act * (1.0 - gate)).astype(BF)
        for h in range(half * HEADS // 2, (half + 1) * HEADS // 2):
            v = acts_ref[:, width + h * each : width + (h + 1) * each]
            q = acts_ref[:, 2 * width + h * each : 2 * width + (h + 1) * each]
            k = acts_ref[:, 3 * width + h * each : 3 * width + (h + 1) * each]
            scores = dot(q, k, 1, 1) * scale
            gate = sigmoid(scores)
            weight = scores * gate
            kept = jnp.where(allowed, weight, 0.0).astype(BF)
            wts_ref[h] = kept
            wslope_ref[h] = jnp.where(allowed, (gate + weight * (1.0 - gate)) * scale, 0.0).astype(BF)
            attended.append(dot(kept, v, 1, 0))
    hat, rstd = norm_parts(jnp.concatenate(attended, axis=1))
    ahat_ref[...] = hat
    arstd_ref[...] = jnp.broadcast_to(rstd, arstd_ref.shape)
    mixed = (hat * acts_ref[:, :width].astype(F32)).astype(BF).T.reshape(32, 2, 16, rows)
    even = core_index() == 0
    keep_ref[...] = jnp.where(even, mixed[:, 0], mixed[:, 1]).reshape(width // 2, rows)
    swap_ref[: width // 2] = jnp.where(even, mixed[:, 1], mixed[:, 0]).reshape(width // 2, rows)
    swap_ref[width // 2 :] = rc_ref[:, 16:32, :].reshape(width, rows)


def mixed_grad_kernel(rc_ref, w_out_ref, d_mixed_ref):
    cots = rc_ref[:, 16:32, :].reshape(-1, LANES)
    d_mixed_ref[...] = dot(cots, w_out_ref[...], 0, 1).astype(BF)


def product_kernel(rc_ref, own_ref, got_ref, order_hbm, *out_refs):
    half = own_ref.shape[0]
    up = 2 * (lax.axis_index("rep") & 1)
    right = (lax.axis_index("col") >> 1) & 1
    mixed = jnp.concatenate([own_ref[...], got_ref[:half]], axis=1)
    for to, out in zip((up + right, 2 - up + right, up + 1 - right, 3 - up - right), out_refs):
        left_part = rc_ref[pl.ds(to * 16, 16), 16:32, :].reshape(256, LANES)
        right_part = got_ref[pl.ds(pl.multiple_of(half + to * 256, 256), 256), :]
        term = dot(mixed, jnp.concatenate([left_part, right_part], axis=1), 1, 1).astype(BF)
        out[:, 0:16, :] = term[:, :LANES].reshape(32, 16, LANES)
        out[:, 16:32, :] = term[:, LANES:].reshape(32, 16, LANES)


def backward_kernel(rc_ref, d_mixed_ref, acts_ref, slope_ref, wts_ref, wslope_ref, ahat_ref, arstd_ref, w_in, keep_ref, swap_ref, d_pre):
    width = rc_ref.shape[0] * 16
    rows = rc_ref.shape[2]
    d_mixed = d_mixed_ref[...].astype(F32)
    hat = ahat_ref[...]
    d_pre[:, :width] = ((d_mixed * hat) * slope_ref[:, :width].astype(F32)).astype(BF)
    d_att = norm_back(hat, arstd_ref[:, 0:1], d_mixed * acts_ref[:, :width].astype(F32)).astype(BF)
    each = width // HEADS
    for h in range(HEADS):
        vs = slice(width + h * each, width + (h + 1) * each)
        qs = slice(2 * width + h * each, 2 * width + (h + 1) * each)
        ks = slice(3 * width + h * each, 3 * width + (h + 1) * each)
        da = d_att[:, h * each : (h + 1) * each]
        d_weight = dot(da, acts_ref[:, vs], 1, 1)
        d_score = (d_weight * wslope_ref[h].astype(F32)).astype(BF)
        d_pre[:, vs] = (dot(wts_ref[h], da, 0, 0) * slope_ref[:, vs].astype(F32)).astype(BF)
        d_pre[:, qs] = (dot(d_score, acts_ref[:, ks], 1, 0) * slope_ref[:, qs].astype(F32)).astype(BF)
        d_pre[:, ks] = (dot(d_score, acts_ref[:, qs], 0, 0) * slope_ref[:, ks].astype(F32)).astype(BF)
    d_normed = dot(d_pre[...], w_in[...], 1, 1)
    cots = rc_ref[:, 16:32, :].reshape(width, rows).T
    x = rc_ref[:, 0:16, :].reshape(width, rows).T
    normed, rstd = norm_parts(x.astype(F32))
    grad = norm_back(normed, rstd, d_normed) + cots.astype(F32)
    grad = grad.astype(BF).T.reshape(32, 2, 16, rows)
    even = core_index() == 0
    keep_ref[...] = jnp.where(even, grad[:, 0], grad[:, 1])
    swap_ref[...] = jnp.where(even, grad[:, 1], grad[:, 0])


def merge_kernel(keep_ref, swapped_ref, *refs):
    out_ref = refs[-1]
    core = core_index()
    out_ref[:, pl.ds(pl.multiple_of(core * 16, 16), 16), :] = keep_ref[...]
    out_ref[:, pl.ds(pl.multiple_of((1 - core) * 16, 16), 16), :] = swapped_ref[...]
    total = refs[0][...].astype(F32)
    for part in refs[1:-1]:
        total += part[...].astype(F32)
    out_ref[:, 32:64, :] = total.astype(BF)


def last_sum_kernel(got_ref, out_ref):
    for side in range(2):
        total = got_ref[side, 32:64, :].astype(F32)
        for i in range(side + 2, got_ref.shape[0], 2):
            total += got_ref[i, 32:64, :].astype(F32)
        out_ref[:, 2 * side * LANES : (2 * side + 1) * LANES] = total[0:16]
        out_ref[:, (2 * side + 1) * LANES : (2 * side + 2) * LANES] = total[16:32]


def join_kernel(mine_ref, one_ref, two_ref, three_ref, out_ref):
    half = mine_ref.shape[1]
    up = lax.axis_index("rep") & 1
    out_ref[:, pl.ds(pl.multiple_of(up * half, half), half)] = mine_ref[...] + two_ref[...]
    out_ref[:, pl.ds(pl.multiple_of((1 - up) * half, half), half)] = one_ref[...] + three_ref[...]


def partners(along_x, along_rep):
    pairs = []
    for i in range(64):
        way = (1, 3)[i % 2]
        for y in range(4):
            to = i ^ (2 * way if along_x else 0), y ^ (way if along_rep else 0)
            pairs.append((i * 4 + y, to[0] * 4 + to[1]))
    return pairs


def per_device(looked, cotangent, w_in, w_out, lengths, owner):
    cols = lax.axis_size("col")
    events, mine_cols = looked.shape
    width = w_out.shape[0]
    rows = events // cols
    users = lengths.shape[0]
    send, table, first = pl.pallas_call(
        pack_kernel,
        out_shape=(
            shape((cols, 2 * mine_cols, rows)),
            shape((4 * users,), jnp.int32),
            shape((16384, LANES), jnp.int32),
        ),
        in_specs=[HBM] * 4,
        out_specs=(VMEM, SMEM, HBM),
        scratch_shapes=[
            pltpu.VMEM((mine_cols, events), BF),
            pltpu.VMEM((mine_cols, events), BF),
            pltpu.SMEM((4, cols), jnp.int32),
            pltpu.SMEM((cols,), jnp.int32),
            pltpu.VMEM((8, LANES), jnp.int32),
            pltpu.SemaphoreType.DMA((5,)),
        ],
        compiler_params=params(60),
    )(lengths, owner, looked.T, cotangent.T)
    packed = lax.all_to_all(send, "col", split_axis=0, concat_axis=0, tiled=True)
    acts, slope, wts, wslope, ahat, arstd, keep, swap = pl.pallas_call(
        forward_kernel,
        out_shape=(
            shape((rows, 4 * width)),
            shape((rows, 4 * width)),
            shape((HEADS, rows, rows)),
            shape((HEADS, rows, rows)),
            shape((rows, width), F32),
            shape((rows, LANES), F32),
            shape((width // 2, rows)),
            shape((width + width // 2, rows)),
        ),
        in_specs=[HBM, VMEM, HBM],
        scratch_shapes=[
            pltpu.VMEM(w_in.shape, BF),
            pltpu.VMEM((8, LANES), jnp.int32),
            pltpu.SemaphoreType.DMA((CHUNKS + 1,)),
        ],
        compiler_params=params(48),
    )(first, packed, w_in)
    other_core = [(i, i ^ 1) for i in range(cols)]
    got = lax.ppermute(swap, "col", other_core)
    d_mixed = pl.pallas_call(mixed_grad_kernel, out_shape=shape((rows, width)), compiler_params=params(16))(packed, w_out)
    block = (cols // 2, 2 * mine_cols, LANES)
    terms = pl.pallas_call(
        product_kernel,
        out_shape=[shape(block)] * 4,
        in_specs=[VMEM, VMEM, VMEM, ANY],
        compiler_params=params(16),
    )(packed, keep, got, d_mixed)
    ways = (False, True), (True, False), (True, True)
    terms = [terms[0]] + [lax.ppermute(t, ("col", "rep"), partners(*way)) for t, way in zip(terms[1:], ways)]
    grad, swap = pl.pallas_call(
        backward_kernel,
        out_shape=[shape((cols // 2, mine_cols, rows))] * 2,
        in_specs=[VMEM] * 9,
        scratch_shapes=[pltpu.VMEM((rows, 4 * width), BF)],
        compiler_params=params(16),
    )(packed, d_mixed, acts, slope, wts, wslope, ahat, arstd, w_in)
    swapped = lax.ppermute(swap, "col", other_core)
    merged = pl.pallas_call(
        merge_kernel,
        out_shape=shape((cols // 2, 4 * mine_cols, rows)),
        in_specs=[VMEM] * 6,
        compiler_params=params(16),
    )(grad, swapped, *terms)
    same_core = [list(range(core, cols, 2)) for core in range(2)]
    back = lax.all_to_all(merged, "col", split_axis=0, concat_axis=0, axis_index_groups=same_core, tiled=True)
    mine = pl.pallas_call(last_sum_kernel, out_shape=shape((mine_cols, width // 2), F32), compiler_params=params(16))(back)
    parts = [mine] + [lax.ppermute(mine, "rep", [(i, i ^ k) for i in range(4)]) for k in range(1, 4)]
    d_looked = pl.pallas_call(
        unpack_kernel,
        out_shape=shape((mine_cols, events)),
        in_specs=[SMEM, VMEM],
        scratch_shapes=[pltpu.VMEM((mine_cols, events + LANES), F32)],
        compiler_params=params(16),
    )(table, back)
    d_w_out = pl.pallas_call(
        join_kernel, out_shape=shape((mine_cols, width), F32), in_specs=[VMEM] * 4, compiler_params=params(16)
    )(*parts)
    return (d_looked.T, d_w_out)


def solution(mesh):
    placed = (P("rep", "col"), P("rep", "col"), P(), P(), P("rep"), P("rep"))
    return jax.shard_map(
        per_device,
        mesh=mesh,
        in_specs=placed,
        out_specs=(P("rep", "col"), P("col", None)),
        check_vma=False,
    )
```

```python
import functools

import jax
import jax.numpy as jnp
from jax import lax
from jax.experimental import pallas as pl
from jax.experimental.pallas import tpu as pltpu
from jax.sharding import PartitionSpec as P

HEADS = 8
EPS = 1e-05
BF = jnp.bfloat16
F32 = jnp.float32
LANES = 128
CHUNKS = 8
IN_FLIGHT = 8
HALVES = ((2, 4, 6), (3, 5, 7))
GATES = (0, 1)
FWD_MIB = 38
USERS_AT_ONCE = 32
OWNERS_AT_ONCE = 8
MOVES_AT_ONCE = 16

SMEM = pl.BlockSpec(memory_space=pltpu.SMEM)
VMEM = pl.BlockSpec(memory_space=pltpu.VMEM)
ANY = pl.BlockSpec(memory_space=pl.ANY)
HBM = pl.BlockSpec(memory_space=pltpu.HBM)


def params(mib):
    return pltpu.CompilerParams(vmem_limit_bytes=mib << 20)


def core_index():
    return lax.axis_index("col") & 1


def shape(dims, dtype=BF):
    return jax.ShapeDtypeStruct(dims, dtype)


def dot(a, b, ca, cb):
    return lax.dot_general(a, b, (((ca,), (cb,)), ((), ())), preferred_element_type=F32)


def pack_kernel(len_hbm, own_hbm, x_hbm, c_hbm, out_ref, table, mine_hbm, x_ref, c_ref, tab, seen, mine, sems):
    users = len_hbm.shape[0]
    lens, owns = table.at[pl.ds(2 * users, users)], table.at[pl.ds(3 * users, users)]
    copies = [
        pltpu.make_async_copy(src, dst, sems.at[i])
        for i, (src, dst) in enumerate(((len_hbm, lens), (own_hbm, owns), (x_hbm, x_ref), (c_hbm, c_ref)))
    ]
    for copy in copies:
        copy.start()
    owners = users // 2
    last = x_ref.shape[1] - LANES
    for j in range(owners):
        seen[j] = 0
    copies[0].wait()
    copies[1].wait()

    def user(u, off):
        own = table[3 * users + u]
        length = table[2 * users + u]
        second = seen[own]
        seen[own] = 1
        start = second * (LANES - length)
        table[u] = off
        table[users + u] = start
        tab[second, own] = off - start
        tab[2 + second, own] = length
        return off + length

    lax.fori_loop(0, users, user, 0, unroll=USERS_AT_ONCE)
    mine[...] = jnp.full(mine.shape, tab[2, lax.axis_index("col")], jnp.int32)
    tell = pltpu.make_async_copy(mine, mine_hbm.at[pl.ds(0, mine.shape[0])], sems.at[4])
    tell.start()
    copies[2].wait()
    copies[3].wait()
    lane = lax.broadcasted_iota(jnp.int32, (16, LANES), 1)

    def owner(j, carry):
        both = []
        for k in range(2):
            first = tab[k, j]
            inside = first & (LANES - 1)
            base = pl.multiple_of(first - inside, LANES)
            after = pl.multiple_of(jnp.minimum(base + LANES, last), LANES)
            back = (LANES - inside) & (LANES - 1)
            low = lane >= inside
            both.append(
                [
                    pltpu.roll(jnp.where(low, ref[:, pl.ds(base, LANES)], ref[:, pl.ds(after, LANES)]), back, 1)
                    for ref in (x_ref, c_ref)
                ]
            )
        head = lane < tab[2, j]
        out_ref[j, 0:16, :] = jnp.where(head, both[0][0], both[1][0])
        out_ref[j, 16:32, :] = jnp.where(head, both[0][1], both[1][1])
        return carry

    lax.fori_loop(0, owners, owner, 0, unroll=OWNERS_AT_ONCE)
    tell.wait()


def unpack_kernel(table, got_ref, out_ref, wide):
    users = table.shape[0] // 4
    lane = lax.broadcasted_iota(jnp.int32, (16, LANES), 1)

    def user(u, carry):
        off = table[u]
        own = table[3 * users + u]
        inside = off & (LANES - 1)
        base = pl.multiple_of(off - inside, LANES)
        turn = (inside - table[users + u]) & (LANES - 1)
        moved = pltpu.roll(got_ref[own >> 1, pl.ds(pl.multiple_of((own & 1) * 16, 16), 16), :], turn, 1).astype(F32)
        end = inside + table[2 * users + u]
        pltpu.store(wide.at[:, pl.ds(base, LANES)], moved, mask=(lane >= inside) & (lane < end))
        pltpu.store(wide.at[:, pl.ds(base + LANES, LANES)], moved, mask=lane < end - LANES)
        return carry

    lax.fori_loop(0, users, user, 0, unroll=MOVES_AT_ONCE)
    out_ref[...] = wide[:, : out_ref.shape[1]].astype(BF)


def sigmoid(v):
    return 0.5 * jnp.tanh(0.5 * v) + 0.5


def norm_parts(v):
    center = v - jnp.mean(v, axis=-1, keepdims=True)
    rstd = lax.rsqrt(jnp.mean(center * center, axis=-1, keepdims=True) + EPS)
    return center * rstd, rstd


def norm_back(hat, rstd, d):
    return rstd * (d - jnp.mean(d, axis=-1, keepdims=True) - hat * jnp.mean(d * hat, axis=-1, keepdims=True))


def column_chunks(w_hbm, w_ref, sems, order):
    per = w_hbm.shape[1] // len(order)

    def copy(i):
        part = pl.ds(order[i] * per, per)
        return pltpu.make_async_copy(w_hbm.at[:, part], w_ref.at[:, part], sems.at[i])

    def start(i):
        if i < len(order):
            copy(i).start()

    def wait(i):
        copy(i).wait()
        start(i + IN_FLIGHT)
        return slice(order[i] * per, (order[i] + 1) * per)

    for i in range(IN_FLIGHT):
        start(i)
    return wait


def forward_kernel(mine_hbm, rc_ref, w_hbm, acts_ref, slope_ref, wts_ref, wslope_ref, ahat_ref, arstd_ref, keep_ref, swap_ref, w_in, mine, sems):
    width = rc_ref.shape[0] * 16
    rows = rc_ref.shape[2]
    tell = pltpu.make_async_copy(mine_hbm.at[pl.ds(0, mine.shape[0])], mine, sems.at[CHUNKS])
    tell.start()
    order = HALVES[0] + HALVES[1] + GATES
    wait = column_chunks(w_hbm, w_in, sems, order)
    x = rc_ref[:, 0:16, :].reshape(width, rows).T
    normed = norm_parts(x.astype(F32))[0].astype(BF)
    query = lax.broadcasted_iota(jnp.int32, (rows, rows), 0)
    key = lax.broadcasted_iota(jnp.int32, (rows, rows), 1)
    tell.wait()
    first = mine[0:1, :]
    allowed = ((query < first) == (key < first)) & (key <= query)
    each = width // HEADS
    scale = float(each) ** -0.5
    attended = []

    def project(*chunks):
        for part in [wait(i) for i in chunks]:
            pre = dot(normed, w_in[:, part], 1, 0)
            gate = sigmoid(pre)
            act = pre * gate
            acts_ref[:, part] = act.astype(BF)
            slope_ref[:, part] = (gate + act * (1.0 - gate)).astype(BF)

    for half in range(2):
        project(*range(3 * half, 3 * half + 3))
        for h in range(half * HEADS // 2, (half + 1) * HEADS // 2):
            v = acts_ref[:, width + h * each : width + (h + 1) * each]
            q = acts_ref[:, 2 * width + h * each : 2 * width + (h + 1) * each]
            k = acts_ref[:, 3 * width + h * each : 3 * width + (h + 1) * each]
            scores = dot(q, k, 1, 1) * scale
            gate = sigmoid(scores)
            weight = scores * gate
            kept = jnp.where(allowed, weight, 0.0).astype(BF)
            wts_ref[h] = kept
            wslope_ref[h] = jnp.where(allowed, (gate + weight * (1.0 - gate)) * scale, 0.0).astype(BF)
            attended.append(dot(kept, v, 1, 0))
    hat, rstd = norm_parts(jnp.concatenate(attended, axis=1))
    ahat_ref[...] = hat
    arstd_ref[...] = jnp.broadcast_to(rstd, arstd_ref.shape)
    project(6, 7)
    mixed = (hat * acts_ref[:, :width].astype(F32)).astype(BF).T.reshape(32, 2, 16, rows)
    even = core_index() == 0
    keep_ref[...] = jnp.where(even, mixed[:, 0], mixed[:, 1]).reshape(width // 2, rows)
    swap_ref[: width // 2] = jnp.where(even, mixed[:, 1], mixed[:, 0]).reshape(width // 2, rows)
    swap_ref[width // 2 :] = rc_ref[:, 16:32, :].reshape(width, rows)


def mixed_grad_kernel(rc_ref, w_out_ref, d_mixed_ref):
    cots = rc_ref[:, 16:32, :].reshape(-1, LANES)
    d_mixed_ref[...] = dot(cots, w_out_ref[...], 0, 1).astype(BF)


def product_kernel(rc_ref, own_ref, got_ref, order_hbm, *out_refs):
    half = own_ref.shape[0]
    up = 2 * (lax.axis_index("rep") & 1)
    right = (lax.axis_index("col") >> 1) & 1
    mixed = jnp.concatenate([own_ref[...], got_ref[:half]], axis=1)
    for to, out in zip((up + right, 3 - up - right, 2 - up + right, up + 1 - right), out_refs):
        left_part = rc_ref[pl.ds(to * 16, 16), 16:32, :].reshape(256, LANES)
        right_part = got_ref[pl.ds(pl.multiple_of(half + to * 256, 256), 256), :]
        term = dot(mixed, jnp.concatenate([left_part, right_part], axis=1), 1, 1).astype(BF)
        out[:, 0:16, :] = term[:, :LANES].reshape(32, 16, LANES)
        out[:, 16:32, :] = term[:, LANES:].reshape(32, 16, LANES)


def backward_kernel(rc_ref, d_mixed_ref, acts_ref, slope_ref, wts_ref, wslope_ref, ahat_ref, arstd_ref, w_in, keep_ref, swap_ref, d_pre):
    width = rc_ref.shape[0] * 16
    rows = rc_ref.shape[2]
    d_mixed = d_mixed_ref[...].astype(F32)
    hat = ahat_ref[...]
    d_pre[:, :width] = ((d_mixed * hat) * slope_ref[:, :width].astype(F32)).astype(BF)
    d_att = norm_back(hat, arstd_ref[:, 0:1], d_mixed * acts_ref[:, :width].astype(F32)).astype(BF)
    each = width // HEADS
    for h in range(HEADS):
        vs = slice(width + h * each, width + (h + 1) * each)
        qs = slice(2 * width + h * each, 2 * width + (h + 1) * each)
        ks = slice(3 * width + h * each, 3 * width + (h + 1) * each)
        da = d_att[:, h * each : (h + 1) * each]
        d_weight = dot(da, acts_ref[:, vs], 1, 1)
        d_score = (d_weight * wslope_ref[h].astype(F32)).astype(BF)
        d_pre[:, vs] = (dot(wts_ref[h], da, 0, 0) * slope_ref[:, vs].astype(F32)).astype(BF)
        d_pre[:, qs] = (dot(d_score, acts_ref[:, ks], 1, 0) * slope_ref[:, qs].astype(F32)).astype(BF)
        d_pre[:, ks] = (dot(d_score, acts_ref[:, qs], 0, 0) * slope_ref[:, ks].astype(F32)).astype(BF)
    d_normed = dot(d_pre[...], w_in[...], 1, 1)
    cots = rc_ref[:, 16:32, :].reshape(width, rows).T
    x = rc_ref[:, 0:16, :].reshape(width, rows).T
    normed, rstd = norm_parts(x.astype(F32))
    grad = norm_back(normed, rstd, d_normed) + cots.astype(F32)
    grad = grad.astype(BF).T.reshape(32, 2, 16, rows)
    even = core_index() == 0
    keep_ref[...] = jnp.where(even, grad[:, 0], grad[:, 1])
    swap_ref[...] = jnp.where(even, grad[:, 1], grad[:, 0])


def merge_kernel(keep_ref, swapped_ref, *refs):
    out_ref = refs[-1]
    core = core_index()
    out_ref[:, pl.ds(pl.multiple_of(core * 16, 16), 16), :] = keep_ref[...]
    out_ref[:, pl.ds(pl.multiple_of((1 - core) * 16, 16), 16), :] = swapped_ref[...]
    total = refs[0][...].astype(F32)
    for part in refs[1:-1]:
        total += part[...].astype(F32)
    out_ref[:, 32:64, :] = total.astype(BF)


def last_sum_kernel(got_ref, out_ref):
    for side in range(2):
        total = got_ref[side, 32:64, :].astype(F32)
        for i in range(side + 2, got_ref.shape[0], 2):
            total += got_ref[i, 32:64, :].astype(F32)
        out_ref[:, 2 * side * LANES : (2 * side + 1) * LANES] = total[0:16]
        out_ref[:, (2 * side + 1) * LANES : (2 * side + 2) * LANES] = total[16:32]


def join_kernel(mine_ref, one_ref, two_ref, three_ref, out_ref):
    half = mine_ref.shape[1]
    up = lax.axis_index("rep") & 1
    out_ref[:, pl.ds(pl.multiple_of(up * half, half), half)] = mine_ref[...] + two_ref[...]
    out_ref[:, pl.ds(pl.multiple_of((1 - up) * half, half), half)] = one_ref[...] + three_ref[...]


def partners(along_x, along_rep):
    pairs = []
    for i in range(64):
        way = (1, 3)[i % 2]
        for y in range(4):
            to = i ^ (2 * way if along_x else 0), y ^ (way if along_rep else 0)
            pairs.append((i * 4 + y, to[0] * 4 + to[1]))
    return pairs


def per_device(looked, cotangent, w_in, w_out, lengths, owner):
    cols = lax.axis_size("col")
    events, mine_cols = looked.shape
    width = w_out.shape[0]
    rows = events // cols
    users = lengths.shape[0]
    send, table, first = pl.pallas_call(
        pack_kernel,
        out_shape=(
            shape((cols, 2 * mine_cols, rows)),
            shape((4 * users,), jnp.int32),
            shape((16384, LANES), jnp.int32),
        ),
        in_specs=[HBM] * 4,
        out_specs=(VMEM, SMEM, HBM),
        scratch_shapes=[
            pltpu.VMEM((mine_cols, events), BF),
            pltpu.VMEM((mine_cols, events), BF),
            pltpu.SMEM((4, cols), jnp.int32),
            pltpu.SMEM((cols,), jnp.int32),
            pltpu.VMEM((8, LANES), jnp.int32),
            pltpu.SemaphoreType.DMA((5,)),
        ],
        compiler_params=params(60),
    )(lengths, owner, looked.T, cotangent.T)
    packed = lax.all_to_all(send, "col", split_axis=0, concat_axis=0, tiled=True)
    acts, slope, wts, wslope, ahat, arstd, keep, swap, w_near = pl.pallas_call(
        forward_kernel,
        out_shape=(
            shape((rows, 4 * width)),
            shape((rows, 4 * width)),
            shape((HEADS, rows, rows)),
            shape((HEADS, rows, rows)),
            shape((rows, width), F32),
            shape((rows, LANES), F32),
            shape((width // 2, rows)),
            shape((width + width // 2, rows)),
            shape(w_in.shape),
        ),
        in_specs=[HBM, VMEM, HBM],
        scratch_shapes=[pltpu.VMEM((8, LANES), jnp.int32), pltpu.SemaphoreType.DMA((CHUNKS + 1,))],
        compiler_params=params(FWD_MIB),
    )(first, packed, w_in)
    other_core = [(i, i ^ 1) for i in range(cols)]
    got = lax.ppermute(swap, "col", other_core)
    d_mixed = pl.pallas_call(mixed_grad_kernel, out_shape=shape((rows, width)), compiler_params=params(16))(packed, w_out)
    block = (cols // 2, 2 * mine_cols, LANES)
    terms = pl.pallas_call(
        product_kernel,
        out_shape=[shape(block)] * 4,
        in_specs=[VMEM, VMEM, VMEM, ANY],
        compiler_params=params(16),
    )(packed, keep, got, d_mixed)
    ways = (True, True), (False, True), (True, False)
    terms = [terms[0]] + [lax.ppermute(t, ("col", "rep"), partners(*way)) for t, way in zip(terms[1:], ways)]
    grad, swap = pl.pallas_call(
        backward_kernel,
        out_shape=[shape((cols // 2, mine_cols, rows))] * 2,
        in_specs=[VMEM] * 9,
        scratch_shapes=[pltpu.VMEM((rows, 4 * width), BF)],
        compiler_params=params(16),
    )(packed, d_mixed, acts, slope, wts, wslope, ahat, arstd, w_near)
    swapped = lax.ppermute(swap, "col", other_core)
    merged = pl.pallas_call(
        merge_kernel,
        out_shape=shape((cols // 2, 4 * mine_cols, rows)),
        in_specs=[VMEM] * 6,
        compiler_params=params(16),
    )(grad, swapped, *terms)
    same_core = [list(range(core, cols, 2)) for core in range(2)]
    back = lax.all_to_all(merged, "col", split_axis=0, concat_axis=0, axis_index_groups=same_core, tiled=True)
    mine = pl.pallas_call(last_sum_kernel, out_shape=shape((mine_cols, width // 2), F32), compiler_params=params(16))(back)
    parts = [mine] + [lax.ppermute(mine, "rep", [(i, i ^ k) for i in range(4)]) for k in range(1, 4)]
    d_looked = pl.pallas_call(
        unpack_kernel,
        out_shape=shape((mine_cols, events)),
        in_specs=[SMEM, VMEM],
        scratch_shapes=[pltpu.VMEM((mine_cols, events + LANES), F32)],
        compiler_params=params(16),
    )(table, back)
    d_w_out = pl.pallas_call(
        join_kernel, out_shape=shape((mine_cols, width), F32), in_specs=[VMEM] * 4, compiler_params=params(16)
    )(*parts)
    return (d_looked.T, d_w_out)


def solution(mesh):
    placed = (P("rep", "col"), P("rep", "col"), P(), P(), P("rep"), P("rep"))
    return jax.shard_map(
        per_device,
        mesh=mesh,
        in_specs=placed,
        out_specs=(P("rep", "col"), P("col", None)),
        check_vma=False,
    )
```

```python
import functools

import jax
import jax.numpy as jnp
from jax import lax
from jax.experimental import pallas as pl
from jax.experimental.pallas import tpu as pltpu
from jax.sharding import PartitionSpec as P

HEADS = 8
EPS = 1e-05
BF = jnp.bfloat16
F32 = jnp.float32
LANES = 128
CHUNKS = 8
IN_FLIGHT = 8
HALVES = ((2, 4, 6), (3, 5, 7))
GATES = (0, 1)
FWD_MIB = 38
USERS_AT_ONCE = 32
OWNERS_AT_ONCE = 8
MOVES_AT_ONCE = 16

SMEM = pl.BlockSpec(memory_space=pltpu.SMEM)
VMEM = pl.BlockSpec(memory_space=pltpu.VMEM)
ANY = pl.BlockSpec(memory_space=pl.ANY)
HBM = pl.BlockSpec(memory_space=pltpu.HBM)


def params(mib):
    return pltpu.CompilerParams(vmem_limit_bytes=mib << 20)


def core_index():
    return lax.axis_index("col") & 1


def shape(dims, dtype=BF):
    return jax.ShapeDtypeStruct(dims, dtype)


def dot(a, b, ca, cb):
    return lax.dot_general(a, b, (((ca,), (cb,)), ((), ())), preferred_element_type=F32)


def pack_kernel(len_hbm, own_hbm, x_hbm, c_hbm, out_ref, table, mine_hbm, x_ref, c_ref, tab, seen, mine, sems):
    users = len_hbm.shape[0]
    lens, owns = table.at[pl.ds(2 * users, users)], table.at[pl.ds(3 * users, users)]
    copies = [
        pltpu.make_async_copy(src, dst, sems.at[i])
        for i, (src, dst) in enumerate(((len_hbm, lens), (own_hbm, owns), (x_hbm, x_ref), (c_hbm, c_ref)))
    ]
    for copy in copies:
        copy.start()
    owners = users // 2
    last = x_ref.shape[1] - LANES
    for j in range(owners):
        seen[j] = 0
    copies[0].wait()
    copies[1].wait()

    def user(u, off):
        own = table[3 * users + u]
        length = table[2 * users + u]
        second = seen[own]
        seen[own] = 1
        start = second * (LANES - length)
        table[u] = off
        table[users + u] = start
        tab[second, own] = off - start
        tab[2 + second, own] = length
        return off + length

    lax.fori_loop(0, users, user, 0, unroll=USERS_AT_ONCE)
    mine[...] = jnp.full(mine.shape, tab[2, lax.axis_index("col")], jnp.int32)
    tell = pltpu.make_async_copy(mine, mine_hbm.at[pl.ds(0, mine.shape[0])], sems.at[4])
    tell.start()
    copies[2].wait()
    copies[3].wait()
    lane = lax.broadcasted_iota(jnp.int32, (16, LANES), 1)

    def owner(j, carry):
        both = []
        for k in range(2):
            first = tab[k, j]
            inside = first & (LANES - 1)
            base = pl.multiple_of(first - inside, LANES)
            after = pl.multiple_of(jnp.minimum(base + LANES, last), LANES)
            back = (LANES - inside) & (LANES - 1)
            low = lane >= inside
            both.append(
                [
                    pltpu.roll(jnp.where(low, ref[:, pl.ds(base, LANES)], ref[:, pl.ds(after, LANES)]), back, 1)
                    for ref in (x_ref, c_ref)
                ]
            )
        head = lane < tab[2, j]
        out_ref[j, 0:16, :] = jnp.where(head, both[0][0], both[1][0])
        out_ref[j, 16:32, :] = jnp.where(head, both[0][1], both[1][1])
        return carry

    lax.fori_loop(0, owners, owner, 0, unroll=OWNERS_AT_ONCE)
    tell.wait()


def unpack_kernel(table, got_ref, out_ref, wide):
    users = table.shape[0] // 4
    lane = lax.broadcasted_iota(jnp.int32, (16, LANES), 1)

    def user(u, carry):
        off = table[u]
        own = table[3 * users + u]
        inside = off & (LANES - 1)
        base = pl.multiple_of(off - inside, LANES)
        turn = (inside - table[users + u]) & (LANES - 1)
        moved = pltpu.roll(got_ref[own >> 1, pl.ds(pl.multiple_of((own & 1) * 16, 16), 16), :], turn, 1).astype(F32)
        end = inside + table[2 * users + u]
        pltpu.store(wide.at[:, pl.ds(base, LANES)], moved, mask=(lane >= inside) & (lane < end))
        pltpu.store(wide.at[:, pl.ds(base + LANES, LANES)], moved, mask=lane < end - LANES)
        return carry

    lax.fori_loop(0, users, user, 0, unroll=MOVES_AT_ONCE)
    out_ref[...] = wide[:, : out_ref.shape[1]].astype(BF)


def sigmoid(v):
    return 0.5 * jnp.tanh(0.5 * v) + 0.5


def norm_parts(v):
    center = v - jnp.mean(v, axis=-1, keepdims=True)
    rstd = lax.rsqrt(jnp.mean(center * center, axis=-1, keepdims=True) + EPS)
    return center * rstd, rstd


def norm_back(hat, rstd, d):
    return rstd * (d - jnp.mean(d, axis=-1, keepdims=True) - hat * jnp.mean(d * hat, axis=-1, keepdims=True))


def column_chunks(w_hbm, w_ref, sems, order):
    per = w_hbm.shape[1] // len(order)

    def copy(i):
        part = pl.ds(order[i] * per, per)
        return pltpu.make_async_copy(w_hbm.at[:, part], w_ref.at[:, part], sems.at[i])

    def start(i):
        if i < len(order):
            copy(i).start()

    def wait(i):
        copy(i).wait()
        start(i + IN_FLIGHT)
        return slice(order[i] * per, (order[i] + 1) * per)

    for i in range(IN_FLIGHT):
        start(i)
    return wait


def forward_kernel(mine_hbm, rc_ref, w_hbm, acts_ref, slope_ref, wts_ref, wslope_ref, ahat_ref, arstd_ref, keep_ref, swap_ref, w_in, mine, sems):
    width = rc_ref.shape[0] * 16
    rows = rc_ref.shape[2]
    tell = pltpu.make_async_copy(mine_hbm.at[pl.ds(0, mine.shape[0])], mine, sems.at[CHUNKS])
    tell.start()
    order = HALVES[0] + HALVES[1] + GATES
    wait = column_chunks(w_hbm, w_in, sems, order)
    x = rc_ref[:, 0:16, :].reshape(width, rows).T
    normed = norm_parts(x.astype(F32))[0].astype(BF)
    query = lax.broadcasted_iota(jnp.int32, (rows, rows), 0)
    key = lax.broadcasted_iota(jnp.int32, (rows, rows), 1)
    tell.wait()
    first = mine[0:1, :]
    allowed = ((query < first) == (key < first)) & (key <= query)
    each = width // HEADS
    scale = float(each) ** -0.5
    attended = []

    def project(*chunks):
        for part in [wait(i) for i in chunks]:
            pre = dot(normed, w_in[:, part], 1, 0)
            gate = sigmoid(pre)
            act = pre * gate
            acts_ref[:, part] = act.astype(BF)
            slope_ref[:, part] = (gate + act * (1.0 - gate)).astype(BF)

    for half in range(2):
        project(*range(3 * half, 3 * half + 3))
        for h in range(half * HEADS // 2, (half + 1) * HEADS // 2):
            v = acts_ref[:, width + h * each : width + (h + 1) * each]
            q = acts_ref[:, 2 * width + h * each : 2 * width + (h + 1) * each]
            k = acts_ref[:, 3 * width + h * each : 3 * width + (h + 1) * each]
            scores = dot(q, k, 1, 1) * scale
            gate = sigmoid(scores)
            weight = scores * gate
            kept = jnp.where(allowed, weight, 0.0).astype(BF)
            wts_ref[h] = kept
            wslope_ref[h] = jnp.where(allowed, (gate + weight * (1.0 - gate)) * scale, 0.0).astype(BF)
            attended.append(dot(kept, v, 1, 0))
    hat, rstd = norm_parts(jnp.concatenate(attended, axis=1))
    ahat_ref[...] = hat
    arstd_ref[...] = jnp.broadcast_to(rstd, arstd_ref.shape)
    project(6, 7)
    mixed = (hat * acts_ref[:, :width].astype(F32)).astype(BF).T.reshape(32, 2, 16, rows)
    even = core_index() == 0
    keep_ref[...] = jnp.where(even, mixed[:, 0], mixed[:, 1]).reshape(width // 2, rows)
    swap_ref[: width // 2] = jnp.where(even, mixed[:, 1], mixed[:, 0]).reshape(width // 2, rows)
    swap_ref[width // 2 :] = rc_ref[:, 16:32, :].reshape(width, rows)


def mixed_grad_kernel(rc_ref, w_out_ref, d_mixed_ref):
    cots = rc_ref[:, 16:32, :].reshape(-1, LANES)
    d_mixed_ref[...] = dot(cots, w_out_ref[...], 0, 1).astype(BF)


def product_kernel(rc_ref, own_ref, got_ref, order_hbm, *out_refs):
    half = own_ref.shape[0]
    up = 2 * (lax.axis_index("rep") & 1)
    right = (lax.axis_index("col") >> 1) & 1
    mixed = jnp.concatenate([own_ref[...], got_ref[:half]], axis=1)
    for to, out in zip((up + right, 3 - up - right, 2 - up + right, up + 1 - right), out_refs):
        left_part = rc_ref[pl.ds(to * 16, 16), 16:32, :].reshape(256, LANES)
        right_part = got_ref[pl.ds(pl.multiple_of(half + to * 256, 256), 256), :]
        term = dot(mixed, jnp.concatenate([left_part, right_part], axis=1), 1, 1).astype(BF)
        out[:, 0:16, :] = term[:, :LANES].reshape(32, 16, LANES)
        out[:, 16:32, :] = term[:, LANES:].reshape(32, 16, LANES)


def backward_kernel(rc_ref, d_mixed_ref, acts_ref, slope_ref, wts_ref, wslope_ref, ahat_ref, arstd_ref, w_in, keep_ref, swap_ref, d_pre):
    width = rc_ref.shape[0] * 16
    rows = rc_ref.shape[2]
    d_mixed = d_mixed_ref[...].astype(F32)
    hat = ahat_ref[...]
    d_pre[:, :width] = ((d_mixed * hat) * slope_ref[:, :width].astype(F32)).astype(BF)
    d_att = norm_back(hat, arstd_ref[:, 0:1], d_mixed * acts_ref[:, :width].astype(F32)).astype(BF)
    each = width // HEADS
    for h in range(HEADS):
        vs = slice(width + h * each, width + (h + 1) * each)
        qs = slice(2 * width + h * each, 2 * width + (h + 1) * each)
        ks = slice(3 * width + h * each, 3 * width + (h + 1) * each)
        da = d_att[:, h * each : (h + 1) * each]
        d_weight = dot(da, acts_ref[:, vs], 1, 1)
        d_score = (d_weight * wslope_ref[h].astype(F32)).astype(BF)
        d_pre[:, vs] = (dot(wts_ref[h], da, 0, 0) * slope_ref[:, vs].astype(F32)).astype(BF)
        d_pre[:, qs] = (dot(d_score, acts_ref[:, ks], 1, 0) * slope_ref[:, qs].astype(F32)).astype(BF)
        d_pre[:, ks] = (dot(d_score, acts_ref[:, qs], 0, 0) * slope_ref[:, ks].astype(F32)).astype(BF)
    d_normed = dot(d_pre[...], w_in[...], 1, 1)
    cots = rc_ref[:, 16:32, :].reshape(width, rows).T
    x = rc_ref[:, 0:16, :].reshape(width, rows).T
    normed, rstd = norm_parts(x.astype(F32))
    grad = norm_back(normed, rstd, d_normed) + cots.astype(F32)
    grad = grad.astype(BF).T.reshape(32, 2, 16, rows)
    even = core_index() == 0
    keep_ref[...] = jnp.where(even, grad[:, 0], grad[:, 1])
    swap_ref[...] = jnp.where(even, grad[:, 1], grad[:, 0])


def merge_kernel(keep_ref, swapped_ref, *refs):
    out_ref = refs[-1]
    core = core_index()
    out_ref[:, pl.ds(pl.multiple_of(core * 16, 16), 16), :] = keep_ref[...]
    out_ref[:, pl.ds(pl.multiple_of((1 - core) * 16, 16), 16), :] = swapped_ref[...]
    total = refs[0][...].astype(F32)
    for part in refs[1:-1]:
        total += part[...].astype(F32)
    out_ref[:, 32:64, :] = total.astype(BF)


def last_sum_kernel(got_ref, out_ref):
    for side in range(2):
        total = got_ref[side, 32:64, :].astype(F32)
        for i in range(side + 2, got_ref.shape[0], 2):
            total += got_ref[i, 32:64, :].astype(F32)
        out_ref[:, 2 * side * LANES : (2 * side + 1) * LANES] = total[0:16]
        out_ref[:, (2 * side + 1) * LANES : (2 * side + 2) * LANES] = total[16:32]


def add_kernel(mine_ref, got_ref, out_ref):
    out_ref[...] = mine_ref[...] + got_ref[...]


def join_kernel(mine_ref, got_ref, out_ref):
    half = mine_ref.shape[1]
    up = lax.axis_index("rep") & 1
    out_ref[:, pl.ds(pl.multiple_of(up * half, half), half)] = mine_ref[...]
    out_ref[:, pl.ds(pl.multiple_of((1 - up) * half, half), half)] = got_ref[...]


def partners(along_x, along_rep):
    pairs = []
    for i in range(64):
        way = (1, 3)[i % 2]
        for y in range(4):
            to = i ^ (2 * way if along_x else 0), y ^ (way if along_rep else 0)
            pairs.append((i * 4 + y, to[0] * 4 + to[1]))
    return pairs


def per_device(looked, cotangent, w_in, w_out, lengths, owner):
    cols = lax.axis_size("col")
    events, mine_cols = looked.shape
    width = w_out.shape[0]
    rows = events // cols
    users = lengths.shape[0]
    send, table, first = pl.pallas_call(
        pack_kernel,
        out_shape=(
            shape((cols, 2 * mine_cols, rows)),
            shape((4 * users,), jnp.int32),
            shape((16384, LANES), jnp.int32),
        ),
        in_specs=[HBM] * 4,
        out_specs=(VMEM, SMEM, HBM),
        scratch_shapes=[
            pltpu.VMEM((mine_cols, events), BF),
            pltpu.VMEM((mine_cols, events), BF),
            pltpu.SMEM((4, cols), jnp.int32),
            pltpu.SMEM((cols,), jnp.int32),
            pltpu.VMEM((8, LANES), jnp.int32),
            pltpu.SemaphoreType.DMA((5,)),
        ],
        compiler_params=params(60),
    )(lengths, owner, looked.T, cotangent.T)
    packed = lax.all_to_all(send, "col", split_axis=0, concat_axis=0, tiled=True)
    acts, slope, wts, wslope, ahat, arstd, keep, swap, w_near = pl.pallas_call(
        forward_kernel,
        out_shape=(
            shape((rows, 4 * width)),
            shape((rows, 4 * width)),
            shape((HEADS, rows, rows)),
            shape((HEADS, rows, rows)),
            shape((rows, width), F32),
            shape((rows, LANES), F32),
            shape((width // 2, rows)),
            shape((width + width // 2, rows)),
            shape(w_in.shape),
        ),
        in_specs=[HBM, VMEM, HBM],
        scratch_shapes=[pltpu.VMEM((8, LANES), jnp.int32), pltpu.SemaphoreType.DMA((CHUNKS + 1,))],
        compiler_params=params(FWD_MIB),
    )(first, packed, w_in)
    other_core = [(i, i ^ 1) for i in range(cols)]
    got = lax.ppermute(swap, "col", other_core)
    d_mixed = pl.pallas_call(mixed_grad_kernel, out_shape=shape((rows, width)), compiler_params=params(16))(packed, w_out)
    block = (cols // 2, 2 * mine_cols, LANES)
    terms = pl.pallas_call(
        product_kernel,
        out_shape=[shape(block)] * 4,
        in_specs=[VMEM, VMEM, VMEM, ANY],
        compiler_params=params(16),
    )(packed, keep, got, d_mixed)
    ways = (True, True), (False, True), (True, False)
    terms = [terms[0]] + [lax.ppermute(t, ("col", "rep"), partners(*way)) for t, way in zip(terms[1:], ways)]
    grad, swap = pl.pallas_call(
        backward_kernel,
        out_shape=[shape((cols // 2, mine_cols, rows))] * 2,
        in_specs=[VMEM] * 9,
        scratch_shapes=[pltpu.VMEM((rows, 4 * width), BF)],
        compiler_params=params(16),
    )(packed, d_mixed, acts, slope, wts, wslope, ahat, arstd, w_near)
    swapped = lax.ppermute(swap, "col", other_core)
    merged = pl.pallas_call(
        merge_kernel,
        out_shape=shape((cols // 2, 4 * mine_cols, rows)),
        in_specs=[VMEM] * 6,
        compiler_params=params(16),
    )(grad, swapped, *terms)
    same_core = [list(range(core, cols, 2)) for core in range(2)]
    back = lax.all_to_all(merged, "col", split_axis=0, concat_axis=0, axis_index_groups=same_core, tiled=True)
    mine = pl.pallas_call(last_sum_kernel, out_shape=shape((mine_cols, width // 2), F32), compiler_params=params(16))(back)
    got = lax.ppermute(mine, "rep", [(i, i ^ 2) for i in range(4)])
    mine = pl.pallas_call(add_kernel, out_shape=shape(mine.shape, F32), compiler_params=params(16))(mine, got)
    got = lax.ppermute(mine, "rep", [(i, i ^ 1) for i in range(4)])
    d_looked = pl.pallas_call(
        unpack_kernel,
        out_shape=shape((mine_cols, events)),
        in_specs=[SMEM, VMEM],
        scratch_shapes=[pltpu.VMEM((mine_cols, events + LANES), F32)],
        compiler_params=params(16),
    )(table, back)
    d_w_out = pl.pallas_call(join_kernel, out_shape=shape((mine_cols, width), F32), compiler_params=params(16))(mine, got)
    return (d_looked.T, d_w_out)


def solution(mesh):
    placed = (P("rep", "col"), P("rep", "col"), P(), P(), P("rep"), P("rep"))
    return jax.shard_map(
        per_device,
        mesh=mesh,
        in_specs=placed,
        out_specs=(P("rep", "col"), P("col", None)),
        check_vma=False,
    )
```

```python
import functools

import jax
import jax.numpy as jnp
from jax import lax
from jax.experimental import pallas as pl
from jax.experimental.pallas import tpu as pltpu
from jax.sharding import PartitionSpec as P

HEADS = 8
EPS = 1e-05
BF = jnp.bfloat16
F32 = jnp.float32
LANES = 128
CHUNKS = 8
IN_FLIGHT = 8
HALVES = ((2, 4, 6), (3, 5, 7))
GATES = (0, 1)
FWD_MIB = 38
USERS_AT_ONCE = 32
OWNERS_AT_ONCE = 8
MOVES_AT_ONCE = 16

SMEM = pl.BlockSpec(memory_space=pltpu.SMEM)
VMEM = pl.BlockSpec(memory_space=pltpu.VMEM)
ANY = pl.BlockSpec(memory_space=pl.ANY)
HBM = pl.BlockSpec(memory_space=pltpu.HBM)


def params(mib):
    return pltpu.CompilerParams(vmem_limit_bytes=mib << 20)


def core_index():
    return lax.axis_index("col") & 1


def shape(dims, dtype=BF):
    return jax.ShapeDtypeStruct(dims, dtype)


def dot(a, b, ca, cb):
    return lax.dot_general(a, b, (((ca,), (cb,)), ((), ())), preferred_element_type=F32)


def pack_kernel(len_hbm, own_hbm, x_hbm, c_hbm, out_ref, table, mine_hbm, x_ref, c_ref, tab, seen, mine, sems):
    users = len_hbm.shape[0]
    lens, owns = table.at[pl.ds(2 * users, users)], table.at[pl.ds(3 * users, users)]
    copies = [
        pltpu.make_async_copy(src, dst, sems.at[i])
        for i, (src, dst) in enumerate(((len_hbm, lens), (own_hbm, owns), (x_hbm, x_ref), (c_hbm, c_ref)))
    ]
    for copy in copies:
        copy.start()
    owners = users // 2
    last = x_ref.shape[1] - LANES
    for j in range(owners):
        seen[j] = 0
    copies[0].wait()
    copies[1].wait()

    def user(u, off):
        own = table[3 * users + u]
        length = table[2 * users + u]
        second = seen[own]
        seen[own] = 1
        start = second * (LANES - length)
        table[u] = off
        table[users + u] = start
        tab[second, own] = off - start
        tab[2 + second, own] = length
        return off + length

    lax.fori_loop(0, users, user, 0, unroll=USERS_AT_ONCE)
    mine[...] = jnp.full(mine.shape, tab[2, lax.axis_index("col")], jnp.int32)
    tell = pltpu.make_async_copy(mine, mine_hbm.at[pl.ds(0, mine.shape[0])], sems.at[4])
    tell.start()
    copies[2].wait()
    copies[3].wait()
    lane = lax.broadcasted_iota(jnp.int32, (16, LANES), 1)

    def owner(j, carry):
        both = []
        for k in range(2):
            first = tab[k, j]
            inside = first & (LANES - 1)
            base = pl.multiple_of(first - inside, LANES)
            after = pl.multiple_of(jnp.minimum(base + LANES, last), LANES)
            back = (LANES - inside) & (LANES - 1)
            low = lane >= inside
            both.append(
                [
                    pltpu.roll(jnp.where(low, ref[:, pl.ds(base, LANES)], ref[:, pl.ds(after, LANES)]), back, 1)
                    for ref in (x_ref, c_ref)
                ]
            )
        head = lane < tab[2, j]
        out_ref[j, 0:16, :] = jnp.where(head, both[0][0], both[1][0])
        out_ref[j, 16:32, :] = jnp.where(head, both[0][1], both[1][1])
        return carry

    lax.fori_loop(0, owners, owner, 0, unroll=OWNERS_AT_ONCE)
    tell.wait()


def unpack_kernel(table, got_ref, out_ref, after_ref, wide):
    after_ref[...] = jnp.zeros(after_ref.shape, F32)
    users = table.shape[0] // 4
    lane = lax.broadcasted_iota(jnp.int32, (16, LANES), 1)

    def user(u, carry):
        off = table[u]
        own = table[3 * users + u]
        inside = off & (LANES - 1)
        base = pl.multiple_of(off - inside, LANES)
        turn = (inside - table[users + u]) & (LANES - 1)
        moved = pltpu.roll(got_ref[own >> 1, pl.ds(pl.multiple_of((own & 1) * 16, 16), 16), :], turn, 1).astype(F32)
        end = inside + table[2 * users + u]
        pltpu.store(wide.at[:, pl.ds(base, LANES)], moved, mask=(lane >= inside) & (lane < end))
        pltpu.store(wide.at[:, pl.ds(base + LANES, LANES)], moved, mask=lane < end - LANES)
        return carry

    lax.fori_loop(0, users, user, 0, unroll=MOVES_AT_ONCE)
    out_ref[...] = wide[:, : out_ref.shape[1]].astype(BF)


def sigmoid(v):
    return 0.5 * jnp.tanh(0.5 * v) + 0.5


def norm_parts(v):
    center = v - jnp.mean(v, axis=-1, keepdims=True)
    rstd = lax.rsqrt(jnp.mean(center * center, axis=-1, keepdims=True) + EPS)
    return center * rstd, rstd


def norm_back(hat, rstd, d):
    return rstd * (d - jnp.mean(d, axis=-1, keepdims=True) - hat * jnp.mean(d * hat, axis=-1, keepdims=True))


def column_chunks(w_hbm, w_ref, sems, order):
    per = w_hbm.shape[1] // len(order)

    def copy(i):
        part = pl.ds(order[i] * per, per)
        return pltpu.make_async_copy(w_hbm.at[:, part], w_ref.at[:, part], sems.at[i])

    def start(i):
        if i < len(order):
            copy(i).start()

    def wait(i):
        copy(i).wait()
        start(i + IN_FLIGHT)
        return slice(order[i] * per, (order[i] + 1) * per)

    for i in range(IN_FLIGHT):
        start(i)
    return wait


def forward_kernel(mine_hbm, rc_ref, w_hbm, acts_ref, slope_ref, wts_ref, wslope_ref, ahat_ref, arstd_ref, keep_ref, swap_ref, w_in, mine, sems):
    width = rc_ref.shape[0] * 16
    rows = rc_ref.shape[2]
    tell = pltpu.make_async_copy(mine_hbm.at[pl.ds(0, mine.shape[0])], mine, sems.at[CHUNKS])
    tell.start()
    order = HALVES[0] + HALVES[1] + GATES
    wait = column_chunks(w_hbm, w_in, sems, order)
    x = rc_ref[:, 0:16, :].reshape(width, rows).T
    normed = norm_parts(x.astype(F32))[0].astype(BF)
    query = lax.broadcasted_iota(jnp.int32, (rows, rows), 0)
    key = lax.broadcasted_iota(jnp.int32, (rows, rows), 1)
    tell.wait()
    first = mine[0:1, :]
    allowed = ((query < first) == (key < first)) & (key <= query)
    each = width // HEADS
    scale = float(each) ** -0.5
    attended = []

    def project(*chunks):
        for part in [wait(i) for i in chunks]:
            pre = dot(normed, w_in[:, part], 1, 0)
            gate = sigmoid(pre)
            act = pre * gate
            acts_ref[:, part] = act.astype(BF)
            slope_ref[:, part] = (gate + act * (1.0 - gate)).astype(BF)

    for half in range(2):
        project(*range(3 * half, 3 * half + 3))
        for h in range(half * HEADS // 2, (half + 1) * HEADS // 2):
            v = acts_ref[:, width + h * each : width + (h + 1) * each]
            q = acts_ref[:, 2 * width + h * each : 2 * width + (h + 1) * each]
            k = acts_ref[:, 3 * width + h * each : 3 * width + (h + 1) * each]
            scores = dot(q, k, 1, 1) * scale
            gate = sigmoid(scores)
            weight = scores * gate
            kept = jnp.where(allowed, weight, 0.0).astype(BF)
            wts_ref[h] = kept
            wslope_ref[h] = jnp.where(allowed, (gate + weight * (1.0 - gate)) * scale, 0.0).astype(BF)
            attended.append(dot(kept, v, 1, 0))
    hat, rstd = norm_parts(jnp.concatenate(attended, axis=1))
    ahat_ref[...] = hat
    arstd_ref[...] = jnp.broadcast_to(rstd, arstd_ref.shape)
    project(6, 7)
    mixed = (hat * acts_ref[:, :width].astype(F32)).astype(BF).T.reshape(32, 2, 16, rows)
    even = core_index() == 0
    keep_ref[...] = jnp.where(even, mixed[:, 0], mixed[:, 1]).reshape(width // 2, rows)
    swap_ref[: width // 2] = jnp.where(even, mixed[:, 1], mixed[:, 0]).reshape(width // 2, rows)
    swap_ref[width // 2 :] = rc_ref[:, 16:32, :].reshape(width, rows)


def mixed_grad_kernel(rc_ref, w_out_ref, d_mixed_ref):
    cots = rc_ref[:, 16:32, :].reshape(-1, LANES)
    d_mixed_ref[...] = dot(cots, w_out_ref[...], 0, 1).astype(BF)


def product_kernel(rc_ref, own_ref, got_ref, order_hbm, *out_refs):
    half = own_ref.shape[0]
    up = 2 * (lax.axis_index("rep") & 1)
    right = (lax.axis_index("col") >> 1) & 1
    mixed = jnp.concatenate([own_ref[...], got_ref[:half]], axis=1)
    for to, out in zip((up + right, 3 - up - right, 2 - up + right, up + 1 - right), out_refs):
        left_part = rc_ref[pl.ds(to * 16, 16), 16:32, :].reshape(256, LANES)
        right_part = got_ref[pl.ds(pl.multiple_of(half + to * 256, 256), 256), :]
        term = dot(mixed, jnp.concatenate([left_part, right_part], axis=1), 1, 1).astype(BF)
        out[:, 0:16, :] = term[:, :LANES].reshape(32, 16, LANES)
        out[:, 16:32, :] = term[:, LANES:].reshape(32, 16, LANES)


def backward_kernel(rc_ref, d_mixed_ref, acts_ref, slope_ref, wts_ref, wslope_ref, ahat_ref, arstd_ref, w_in, keep_ref, swap_ref, d_pre):
    width = rc_ref.shape[0] * 16
    rows = rc_ref.shape[2]
    d_mixed = d_mixed_ref[...].astype(F32)
    hat = ahat_ref[...]
    d_pre[:, :width] = ((d_mixed * hat) * slope_ref[:, :width].astype(F32)).astype(BF)
    d_att = norm_back(hat, arstd_ref[:, 0:1], d_mixed * acts_ref[:, :width].astype(F32)).astype(BF)
    each = width // HEADS
    for h in range(HEADS):
        vs = slice(width + h * each, width + (h + 1) * each)
        qs = slice(2 * width + h * each, 2 * width + (h + 1) * each)
        ks = slice(3 * width + h * each, 3 * width + (h + 1) * each)
        da = d_att[:, h * each : (h + 1) * each]
        d_weight = dot(da, acts_ref[:, vs], 1, 1)
        d_score = (d_weight * wslope_ref[h].astype(F32)).astype(BF)
        d_pre[:, vs] = (dot(wts_ref[h], da, 0, 0) * slope_ref[:, vs].astype(F32)).astype(BF)
        d_pre[:, qs] = (dot(d_score, acts_ref[:, ks], 1, 0) * slope_ref[:, qs].astype(F32)).astype(BF)
        d_pre[:, ks] = (dot(d_score, acts_ref[:, qs], 0, 0) * slope_ref[:, ks].astype(F32)).astype(BF)
    d_normed = dot(d_pre[...], w_in[...], 1, 1)
    cots = rc_ref[:, 16:32, :].reshape(width, rows).T
    x = rc_ref[:, 0:16, :].reshape(width, rows).T
    normed, rstd = norm_parts(x.astype(F32))
    grad = norm_back(normed, rstd, d_normed) + cots.astype(F32)
    grad = grad.astype(BF).T.reshape(32, 2, 16, rows)
    even = core_index() == 0
    keep_ref[...] = jnp.where(even, grad[:, 0], grad[:, 1])
    swap_ref[...] = jnp.where(even, grad[:, 1], grad[:, 0])


def merge_kernel(keep_ref, swapped_ref, *refs):
    out_ref = refs[-1]
    core = core_index()
    out_ref[:, pl.ds(pl.multiple_of(core * 16, 16), 16), :] = keep_ref[...]
    out_ref[:, pl.ds(pl.multiple_of((1 - core) * 16, 16), 16), :] = swapped_ref[...]
    total = refs[0][...].astype(F32)
    for part in refs[1:-1]:
        total += part[...].astype(F32)
    out_ref[:, 32:64, :] = total.astype(BF)


def last_sum_kernel(got_ref, out_ref):
    for side in range(2):
        total = got_ref[side, 32:64, :].astype(F32)
        for i in range(side + 2, got_ref.shape[0], 2):
            total += got_ref[i, 32:64, :].astype(F32)
        out_ref[:, 2 * side * LANES : (2 * side + 1) * LANES] = total[0:16]
        out_ref[:, (2 * side + 1) * LANES : (2 * side + 2) * LANES] = total[16:32]


def add_kernel(mine_ref, got_ref, after_ref, out_ref):
    out_ref[...] = mine_ref[...] + got_ref[...]


def join_kernel(mine_ref, got_ref, out_ref):
    half = mine_ref.shape[1]
    up = lax.axis_index("rep") & 1
    out_ref[:, pl.ds(pl.multiple_of(up * half, half), half)] = mine_ref[...]
    out_ref[:, pl.ds(pl.multiple_of((1 - up) * half, half), half)] = got_ref[...]


def partners(along_x, along_rep):
    pairs = []
    for i in range(64):
        way = (1, 3)[i % 2]
        for y in range(4):
            to = i ^ (2 * way if along_x else 0), y ^ (way if along_rep else 0)
            pairs.append((i * 4 + y, to[0] * 4 + to[1]))
    return pairs


def per_device(looked, cotangent, w_in, w_out, lengths, owner):
    cols = lax.axis_size("col")
    events, mine_cols = looked.shape
    width = w_out.shape[0]
    rows = events // cols
    users = lengths.shape[0]
    send, table, first = pl.pallas_call(
        pack_kernel,
        out_shape=(
            shape((cols, 2 * mine_cols, rows)),
            shape((4 * users,), jnp.int32),
            shape((16384, LANES), jnp.int32),
        ),
        in_specs=[HBM] * 4,
        out_specs=(VMEM, SMEM, HBM),
        scratch_shapes=[
            pltpu.VMEM((mine_cols, events), BF),
            pltpu.VMEM((mine_cols, events), BF),
            pltpu.SMEM((4, cols), jnp.int32),
            pltpu.SMEM((cols,), jnp.int32),
            pltpu.VMEM((8, LANES), jnp.int32),
            pltpu.SemaphoreType.DMA((5,)),
        ],
        compiler_params=params(60),
    )(lengths, owner, looked.T, cotangent.T)
    packed = lax.all_to_all(send, "col", split_axis=0, concat_axis=0, tiled=True)
    acts, slope, wts, wslope, ahat, arstd, keep, swap, w_near = pl.pallas_call(
        forward_kernel,
        out_shape=(
            shape((rows, 4 * width)),
            shape((rows, 4 * width)),
            shape((HEADS, rows, rows)),
            shape((HEADS, rows, rows)),
            shape((rows, width), F32),
            shape((rows, LANES), F32),
            shape((width // 2, rows)),
            shape((width + width // 2, rows)),
            shape(w_in.shape),
        ),
        in_specs=[HBM, VMEM, HBM],
        scratch_shapes=[pltpu.VMEM((8, LANES), jnp.int32), pltpu.SemaphoreType.DMA((CHUNKS + 1,))],
        compiler_params=params(FWD_MIB),
    )(first, packed, w_in)
    other_core = [(i, i ^ 1) for i in range(cols)]
    got = lax.ppermute(swap, "col", other_core)
    d_mixed = pl.pallas_call(mixed_grad_kernel, out_shape=shape((rows, width)), compiler_params=params(16))(packed, w_out)
    block = (cols // 2, 2 * mine_cols, LANES)
    terms = pl.pallas_call(
        product_kernel,
        out_shape=[shape(block)] * 4,
        in_specs=[VMEM, VMEM, VMEM, ANY],
        compiler_params=params(16),
    )(packed, keep, got, d_mixed)
    ways = (True, True), (False, True), (True, False)
    terms = [terms[0]] + [lax.ppermute(t, ("col", "rep"), partners(*way)) for t, way in zip(terms[1:], ways)]
    grad, swap = pl.pallas_call(
        backward_kernel,
        out_shape=[shape((cols // 2, mine_cols, rows))] * 2,
        in_specs=[VMEM] * 9,
        scratch_shapes=[pltpu.VMEM((rows, 4 * width), BF)],
        compiler_params=params(16),
    )(packed, d_mixed, acts, slope, wts, wslope, ahat, arstd, w_near)
    swapped = lax.ppermute(swap, "col", other_core)
    merged = pl.pallas_call(
        merge_kernel,
        out_shape=shape((cols // 2, 4 * mine_cols, rows)),
        in_specs=[VMEM] * 6,
        compiler_params=params(16),
    )(grad, swapped, *terms)
    same_core = [list(range(core, cols, 2)) for core in range(2)]
    back = lax.all_to_all(merged, "col", split_axis=0, concat_axis=0, axis_index_groups=same_core, tiled=True)
    mine = pl.pallas_call(last_sum_kernel, out_shape=shape((mine_cols, width // 2), F32), compiler_params=params(16))(back)
    got = lax.ppermute(mine, "rep", [(i, i ^ 2) for i in range(4)])
    d_looked, after = pl.pallas_call(
        unpack_kernel,
        out_shape=(shape((mine_cols, events)), shape((8, LANES), F32)),
        in_specs=[SMEM, VMEM],
        scratch_shapes=[pltpu.VMEM((mine_cols, events + LANES), F32)],
        compiler_params=params(16),
    )(table, back)
    mine = pl.pallas_call(add_kernel, out_shape=shape(mine.shape, F32), compiler_params=params(16))(mine, got, after)
    got = lax.ppermute(mine, "rep", [(i, i ^ 1) for i in range(4)])
    d_w_out = pl.pallas_call(join_kernel, out_shape=shape((mine_cols, width), F32), compiler_params=params(16))(mine, got)
    return (d_looked.T, d_w_out)


def solution(mesh):
    placed = (P("rep", "col"), P("rep", "col"), P(), P(), P("rep"), P("rep"))
    return jax.shard_map(
        per_device,
        mesh=mesh,
        in_specs=placed,
        out_specs=(P("rep", "col"), P("col", None)),
        check_vma=False,
    )
```

```python
import functools

import jax
import jax.numpy as jnp
from jax import lax
from jax.experimental import pallas as pl
from jax.experimental.pallas import tpu as pltpu
from jax.sharding import PartitionSpec as P

HEADS = 8
EPS = 1e-05
BF = jnp.bfloat16
F32 = jnp.float32
LANES = 128
CHUNKS = 8
IN_FLIGHT = 8
HALVES = ((2, 4, 6), (3, 5, 7))
GATES = (0, 1)
FWD_MIB = 38
USERS_AT_ONCE = 32
OWNERS_AT_ONCE = 8
MOVES_AT_ONCE = 16

SMEM = pl.BlockSpec(memory_space=pltpu.SMEM)
VMEM = pl.BlockSpec(memory_space=pltpu.VMEM)
ANY = pl.BlockSpec(memory_space=pl.ANY)
HBM = pl.BlockSpec(memory_space=pltpu.HBM)


def params(mib):
    return pltpu.CompilerParams(vmem_limit_bytes=mib << 20)


def core_index():
    return lax.axis_index("col") & 1


def shape(dims, dtype=BF):
    return jax.ShapeDtypeStruct(dims, dtype)


def dot(a, b, ca, cb):
    return lax.dot_general(a, b, (((ca,), (cb,)), ((), ())), preferred_element_type=F32)


def pack_kernel(len_hbm, own_hbm, x_hbm, c_hbm, out_ref, table, mine_hbm, x_ref, c_ref, tab, seen, mine, sems):
    users = len_hbm.shape[0]
    lens, owns = table.at[pl.ds(2 * users, users)], table.at[pl.ds(3 * users, users)]
    copies = [
        pltpu.make_async_copy(src, dst, sems.at[i])
        for i, (src, dst) in enumerate(((len_hbm, lens), (own_hbm, owns), (x_hbm, x_ref), (c_hbm, c_ref)))
    ]
    for copy in copies:
        copy.start()
    owners = users // 2
    last = x_ref.shape[1] - LANES
    for j in range(owners):
        seen[j] = 0
    copies[0].wait()
    copies[1].wait()

    def user(u, off):
        own = table[3 * users + u]
        length = table[2 * users + u]
        second = seen[own]
        seen[own] = 1
        start = second * (LANES - length)
        table[u] = off
        table[users + u] = start
        tab[second, own] = off - start
        tab[2 + second, own] = length
        return off + length

    lax.fori_loop(0, users, user, 0, unroll=USERS_AT_ONCE)
    mine[...] = jnp.full(mine.shape, tab[2, lax.axis_index("col")], jnp.int32)
    tell = pltpu.make_async_copy(mine, mine_hbm.at[pl.ds(0, mine.shape[0])], sems.at[4])
    tell.start()
    copies[2].wait()
    copies[3].wait()
    lane = lax.broadcasted_iota(jnp.int32, (16, LANES), 1)

    def owner(j, carry):
        both = []
        for k in range(2):
            first = tab[k, j]
            inside = first & (LANES - 1)
            base = pl.multiple_of(first - inside, LANES)
            after = pl.multiple_of(jnp.minimum(base + LANES, last), LANES)
            back = (LANES - inside) & (LANES - 1)
            low = lane >= inside
            both.append(
                [
                    pltpu.roll(jnp.where(low, ref[:, pl.ds(base, LANES)], ref[:, pl.ds(after, LANES)]), back, 1)
                    for ref in (x_ref, c_ref)
                ]
            )
        head = lane < tab[2, j]
        out_ref[j, 0:16, :] = jnp.where(head, both[0][0], both[1][0])
        out_ref[j, 16:32, :] = jnp.where(head, both[0][1], both[1][1])
        return carry

    lax.fori_loop(0, owners, owner, 0, unroll=OWNERS_AT_ONCE)
    tell.wait()


def unpack_kernel(table, got_ref, out_ref, wide):
    users = table.shape[0] // 4
    lane = lax.broadcasted_iota(jnp.int32, (16, LANES), 1)

    def user(u, carry):
        off = table[u]
        own = table[3 * users + u]
        inside = off & (LANES - 1)
        base = pl.multiple_of(off - inside, LANES)
        turn = (inside - table[users + u]) & (LANES - 1)
        moved = pltpu.roll(got_ref[own >> 1, pl.ds(pl.multiple_of((own & 1) * 16, 16), 16), :], turn, 1).astype(F32)
        end = inside + table[2 * users + u]
        pltpu.store(wide.at[:, pl.ds(base, LANES)], moved, mask=(lane >= inside) & (lane < end))
        pltpu.store(wide.at[:, pl.ds(base + LANES, LANES)], moved, mask=lane < end - LANES)
        return carry

    lax.fori_loop(0, users, user, 0, unroll=MOVES_AT_ONCE)
    out_ref[...] = wide[:, : out_ref.shape[1]].astype(BF)


def sigmoid(v):
    return 0.5 * jnp.tanh(0.5 * v) + 0.5


def norm_parts(v):
    center = v - jnp.mean(v, axis=-1, keepdims=True)
    rstd = lax.rsqrt(jnp.mean(center * center, axis=-1, keepdims=True) + EPS)
    return center * rstd, rstd


def norm_back(hat, rstd, d):
    return rstd * (d - jnp.mean(d, axis=-1, keepdims=True) - hat * jnp.mean(d * hat, axis=-1, keepdims=True))


def column_chunks(w_hbm, w_ref, sems, order):
    per = w_hbm.shape[1] // len(order)

    def copy(i):
        part = pl.ds(order[i] * per, per)
        return pltpu.make_async_copy(w_hbm.at[:, part], w_ref.at[:, part], sems.at[i])

    def start(i):
        if i < len(order):
            copy(i).start()

    def wait(i):
        copy(i).wait()
        start(i + IN_FLIGHT)
        return slice(order[i] * per, (order[i] + 1) * per)

    for i in range(IN_FLIGHT):
        start(i)
    return wait


def forward_kernel(mine_hbm, rc_ref, w_hbm, acts_ref, slope_ref, wts_ref, wslope_ref, ahat_ref, arstd_ref, keep_ref, swap_ref, w_in, mine, sems):
    width = rc_ref.shape[0] * 16
    rows = rc_ref.shape[2]
    tell = pltpu.make_async_copy(mine_hbm.at[pl.ds(0, mine.shape[0])], mine, sems.at[CHUNKS])
    tell.start()
    order = HALVES[0] + HALVES[1] + GATES
    wait = column_chunks(w_hbm, w_in, sems, order)
    x = rc_ref[:, 0:16, :].reshape(width, rows).T
    normed = norm_parts(x.astype(F32))[0].astype(BF)
    query = lax.broadcasted_iota(jnp.int32, (rows, rows), 0)
    key = lax.broadcasted_iota(jnp.int32, (rows, rows), 1)
    tell.wait()
    first = mine[0:1, :]
    allowed = ((query < first) == (key < first)) & (key <= query)
    each = width // HEADS
    scale = float(each) ** -0.5
    attended = []

    def project(*chunks):
        for part in [wait(i) for i in chunks]:
            pre = dot(normed, w_in[:, part], 1, 0)
            gate = sigmoid(pre)
            act = pre * gate
            acts_ref[:, part] = act.astype(BF)
            slope_ref[:, part] = (gate + act * (1.0 - gate)).astype(BF)

    for half in range(2):
        project(*range(3 * half, 3 * half + 3))
        for h in range(half * HEADS // 2, (half + 1) * HEADS // 2):
            v = acts_ref[:, width + h * each : width + (h + 1) * each]
            q = acts_ref[:, 2 * width + h * each : 2 * width + (h + 1) * each]
            k = acts_ref[:, 3 * width + h * each : 3 * width + (h + 1) * each]
            scores = dot(q, k, 1, 1) * scale
            gate = sigmoid(scores)
            weight = scores * gate
            kept = jnp.where(allowed, weight, 0.0).astype(BF)
            wts_ref[h] = kept
            wslope_ref[h] = jnp.where(allowed, (gate + weight * (1.0 - gate)) * scale, 0.0).astype(BF)
            attended.append(dot(kept, v, 1, 0))
    hat, rstd = norm_parts(jnp.concatenate(attended, axis=1))
    ahat_ref[...] = hat
    arstd_ref[...] = jnp.broadcast_to(rstd, arstd_ref.shape)
    project(6, 7)
    mixed = (hat * acts_ref[:, :width].astype(F32)).astype(BF).T.reshape(32, 2, 16, rows)
    even = core_index() == 0
    keep_ref[...] = jnp.where(even, mixed[:, 0], mixed[:, 1]).reshape(width // 2, rows)
    swap_ref[: width // 2] = jnp.where(even, mixed[:, 1], mixed[:, 0]).reshape(width // 2, rows)
    swap_ref[width // 2 :] = rc_ref[:, 16:32, :].reshape(width, rows)


def mixed_grad_kernel(rc_ref, w_out_ref, d_mixed_ref):
    cots = rc_ref[:, 16:32, :].reshape(-1, LANES)
    d_mixed_ref[...] = dot(cots, w_out_ref[...], 0, 1).astype(BF)


def product_kernel(rc_ref, own_ref, got_ref, order_hbm, *out_refs):
    half = own_ref.shape[0]
    up = 2 * (lax.axis_index("rep") & 1)
    right = (lax.axis_index("col") >> 1) & 1
    mixed = jnp.concatenate([own_ref[...], got_ref[:half]], axis=1)
    for to, out in zip((up + right, 3 - up - right, 2 - up + right, up + 1 - right), out_refs):
        left_part = rc_ref[pl.ds(to * 16, 16), 16:32, :].reshape(256, LANES)
        right_part = got_ref[pl.ds(pl.multiple_of(half + to * 256, 256), 256), :]
        term = dot(mixed, jnp.concatenate([left_part, right_part], axis=1), 1, 1).astype(BF)
        out[:, 0:16, :] = term[:, :LANES].reshape(32, 16, LANES)
        out[:, 16:32, :] = term[:, LANES:].reshape(32, 16, LANES)


def backward_kernel(rc_ref, d_mixed_ref, acts_ref, slope_ref, wts_ref, wslope_ref, ahat_ref, arstd_ref, w_in, keep_ref, swap_ref, d_pre):
    width = rc_ref.shape[0] * 16
    rows = rc_ref.shape[2]
    d_mixed = d_mixed_ref[...].astype(F32)
    hat = ahat_ref[...]
    d_pre[:, :width] = ((d_mixed * hat) * slope_ref[:, :width].astype(F32)).astype(BF)
    d_att = norm_back(hat, arstd_ref[:, 0:1], d_mixed * acts_ref[:, :width].astype(F32)).astype(BF)
    each = width // HEADS
    for h in range(HEADS):
        vs = slice(width + h * each, width + (h + 1) * each)
        qs = slice(2 * width + h * each, 2 * width + (h + 1) * each)
        ks = slice(3 * width + h * each, 3 * width + (h + 1) * each)
        da = d_att[:, h * each : (h + 1) * each]
        d_weight = dot(da, acts_ref[:, vs], 1, 1)
        d_score = (d_weight * wslope_ref[h].astype(F32)).astype(BF)
        d_pre[:, vs] = (dot(wts_ref[h], da, 0, 0) * slope_ref[:, vs].astype(F32)).astype(BF)
        d_pre[:, qs] = (dot(d_score, acts_ref[:, ks], 1, 0) * slope_ref[:, qs].astype(F32)).astype(BF)
        d_pre[:, ks] = (dot(d_score, acts_ref[:, qs], 0, 0) * slope_ref[:, ks].astype(F32)).astype(BF)
    d_normed = dot(d_pre[...], w_in[...], 1, 1)
    cots = rc_ref[:, 16:32, :].reshape(width, rows).T
    x = rc_ref[:, 0:16, :].reshape(width, rows).T
    normed, rstd = norm_parts(x.astype(F32))
    grad = norm_back(normed, rstd, d_normed) + cots.astype(F32)
    grad = grad.astype(BF).T.reshape(32, 2, 16, rows)
    even = core_index() == 0
    keep_ref[...] = jnp.where(even, grad[:, 0], grad[:, 1])
    swap_ref[...] = jnp.where(even, grad[:, 1], grad[:, 0])


def merge_kernel(keep_ref, swapped_ref, *refs):
    out_ref = refs[-1]
    core = core_index()
    out_ref[:, pl.ds(pl.multiple_of(core * 16, 16), 16), :] = keep_ref[...]
    out_ref[:, pl.ds(pl.multiple_of((1 - core) * 16, 16), 16), :] = swapped_ref[...]
    total = refs[0][...].astype(F32)
    for part in refs[1:-1]:
        total += part[...].astype(F32)
    out_ref[:, 32:64, :] = total.astype(BF)


def last_sum_kernel(got_ref, out_ref):
    for side in range(2):
        total = got_ref[side, 32:64, :].astype(F32)
        for i in range(side + 2, got_ref.shape[0], 2):
            total += got_ref[i, 32:64, :].astype(F32)
        out_ref[:, 2 * side * LANES : (2 * side + 1) * LANES] = total[0:16]
        out_ref[:, (2 * side + 1) * LANES : (2 * side + 2) * LANES] = total[16:32]


def join_kernel(mine_ref, three_ref, two_ref, one_ref, out_ref):
    half = mine_ref.shape[1]
    up = lax.axis_index("rep") & 1
    out_ref[:, pl.ds(pl.multiple_of(up * half, half), half)] = mine_ref[...] + two_ref[...]
    out_ref[:, pl.ds(pl.multiple_of((1 - up) * half, half), half)] = one_ref[...] + three_ref[...]


def partners(along_x, along_rep):
    pairs = []
    for i in range(64):
        way = (1, 3)[i % 2]
        for y in range(4):
            to = i ^ (2 * way if along_x else 0), y ^ (way if along_rep else 0)
            pairs.append((i * 4 + y, to[0] * 4 + to[1]))
    return pairs


def per_device(looked, cotangent, w_in, w_out, lengths, owner):
    cols = lax.axis_size("col")
    events, mine_cols = looked.shape
    width = w_out.shape[0]
    rows = events // cols
    users = lengths.shape[0]
    send, table, first = pl.pallas_call(
        pack_kernel,
        out_shape=(
            shape((cols, 2 * mine_cols, rows)),
            shape((4 * users,), jnp.int32),
            shape((16384, LANES), jnp.int32),
        ),
        in_specs=[HBM] * 4,
        out_specs=(VMEM, SMEM, HBM),
        scratch_shapes=[
            pltpu.VMEM((mine_cols, events), BF),
            pltpu.VMEM((mine_cols, events), BF),
            pltpu.SMEM((4, cols), jnp.int32),
            pltpu.SMEM((cols,), jnp.int32),
            pltpu.VMEM((8, LANES), jnp.int32),
            pltpu.SemaphoreType.DMA((5,)),
        ],
        compiler_params=params(60),
    )(lengths, owner, looked.T, cotangent.T)
    packed = lax.all_to_all(send, "col", split_axis=0, concat_axis=0, tiled=True)
    acts, slope, wts, wslope, ahat, arstd, keep, swap, w_near = pl.pallas_call(
        forward_kernel,
        out_shape=(
            shape((rows, 4 * width)),
            shape((rows, 4 * width)),
            shape((HEADS, rows, rows)),
            shape((HEADS, rows, rows)),
            shape((rows, width), F32),
            shape((rows, LANES), F32),
            shape((width // 2, rows)),
            shape((width + width // 2, rows)),
            shape(w_in.shape),
        ),
        in_specs=[HBM, VMEM, HBM],
        scratch_shapes=[pltpu.VMEM((8, LANES), jnp.int32), pltpu.SemaphoreType.DMA((CHUNKS + 1,))],
        compiler_params=params(FWD_MIB),
    )(first, packed, w_in)
    other_core = [(i, i ^ 1) for i in range(cols)]
    got = lax.ppermute(swap, "col", other_core)
    d_mixed = pl.pallas_call(mixed_grad_kernel, out_shape=shape((rows, width)), compiler_params=params(16))(packed, w_out)
    block = (cols // 2, 2 * mine_cols, LANES)
    terms = pl.pallas_call(
        product_kernel,
        out_shape=[shape(block)] * 4,
        in_specs=[VMEM, VMEM, VMEM, ANY],
        compiler_params=params(16),
    )(packed, keep, got, d_mixed)
    ways = (True, True), (False, True), (True, False)
    terms = [terms[0]] + [lax.ppermute(t, ("col", "rep"), partners(*way)) for t, way in zip(terms[1:], ways)]
    grad, swap = pl.pallas_call(
        backward_kernel,
        out_shape=[shape((cols // 2, mine_cols, rows))] * 2,
        in_specs=[VMEM] * 9,
        scratch_shapes=[pltpu.VMEM((rows, 4 * width), BF)],
        compiler_params=params(16),
    )(packed, d_mixed, acts, slope, wts, wslope, ahat, arstd, w_near)
    swapped = lax.ppermute(swap, "col", other_core)
    merged = pl.pallas_call(
        merge_kernel,
        out_shape=shape((cols // 2, 4 * mine_cols, rows)),
        in_specs=[VMEM] * 6,
        compiler_params=params(16),
    )(grad, swapped, *terms)
    same_core = [list(range(core, cols, 2)) for core in range(2)]
    back = lax.all_to_all(merged, "col", split_axis=0, concat_axis=0, axis_index_groups=same_core, tiled=True)
    mine = pl.pallas_call(last_sum_kernel, out_shape=shape((mine_cols, width // 2), F32), compiler_params=params(16))(back)
    three, two, one = [lax.ppermute(mine, "rep", [(i, i ^ k) for i in range(4)]) for k in (3, 2, 1)]
    d_looked = pl.pallas_call(
        unpack_kernel,
        out_shape=shape((mine_cols, events)),
        in_specs=[SMEM, VMEM],
        scratch_shapes=[pltpu.VMEM((mine_cols, events + LANES), F32)],
        compiler_params=params(16),
    )(table, back)
    d_w_out = pl.pallas_call(
        join_kernel, out_shape=shape((mine_cols, width), F32), in_specs=[VMEM] * 4, compiler_params=params(16)
    )(mine, three, two, one)
    return (d_looked.T, d_w_out)


def solution(mesh):
    placed = (P("rep", "col"), P("rep", "col"), P(), P(), P("rep"), P("rep"))
    return jax.shard_map(
        per_device,
        mesh=mesh,
        in_specs=placed,
        out_specs=(P("rep", "col"), P("col", None)),
        check_vma=False,
    )
```

```python
import functools

import jax
import jax.numpy as jnp
from jax import lax
from jax.experimental import pallas as pl
from jax.experimental.pallas import tpu as pltpu
from jax.sharding import PartitionSpec as P

HEADS = 8
EPS = 1e-05
BF = jnp.bfloat16
F32 = jnp.float32
LANES = 128
CHUNKS = 8
IN_FLIGHT = 8
HALVES = ((2, 4, 6), (3, 5, 7))
GATES = (0, 1)
FWD_MIB = 38
USERS_AT_ONCE = 32
OWNERS_AT_ONCE = 8
MOVES_AT_ONCE = 16

SMEM = pl.BlockSpec(memory_space=pltpu.SMEM)
VMEM = pl.BlockSpec(memory_space=pltpu.VMEM)
ANY = pl.BlockSpec(memory_space=pl.ANY)
HBM = pl.BlockSpec(memory_space=pltpu.HBM)


def params(mib):
    return pltpu.CompilerParams(vmem_limit_bytes=mib << 20)


def core_index():
    return lax.axis_index("col") & 1


def shape(dims, dtype=BF):
    return jax.ShapeDtypeStruct(dims, dtype)


def dot(a, b, ca, cb):
    return lax.dot_general(a, b, (((ca,), (cb,)), ((), ())), preferred_element_type=F32)


def pack_kernel(len_hbm, own_hbm, x_hbm, c_hbm, out_ref, table, mine_hbm, x_ref, c_ref, tab, seen, mine, sems):
    users = len_hbm.shape[0]
    lens, owns = table.at[pl.ds(2 * users, users)], table.at[pl.ds(3 * users, users)]
    copies = [
        pltpu.make_async_copy(src, dst, sems.at[i])
        for i, (src, dst) in enumerate(((len_hbm, lens), (own_hbm, owns), (x_hbm, x_ref), (c_hbm, c_ref)))
    ]
    for copy in copies:
        copy.start()
    owners = users // 2
    last = x_ref.shape[1] - LANES
    for j in range(owners):
        seen[j] = 0
    copies[0].wait()
    copies[1].wait()

    def user(u, off):
        own = table[3 * users + u]
        length = table[2 * users + u]
        second = seen[own]
        seen[own] = 1
        start = second * (LANES - length)
        table[u] = off
        table[users + u] = start
        tab[second, own] = off - start
        tab[2 + second, own] = length
        return off + length

    lax.fori_loop(0, users, user, 0, unroll=USERS_AT_ONCE)
    mine[...] = jnp.full(mine.shape, tab[2, lax.axis_index("col")], jnp.int32)
    tell = pltpu.make_async_copy(mine, mine_hbm.at[pl.ds(0, mine.shape[0])], sems.at[4])
    tell.start()
    copies[2].wait()
    copies[3].wait()
    lane = lax.broadcasted_iota(jnp.int32, (16, LANES), 1)

    def owner(j, carry):
        both = []
        for k in range(2):
            first = tab[k, j]
            inside = first & (LANES - 1)
            base = pl.multiple_of(first - inside, LANES)
            after = pl.multiple_of(jnp.minimum(base + LANES, last), LANES)
            back = (LANES - inside) & (LANES - 1)
            low = lane >= inside
            both.append(
                [
                    pltpu.roll(jnp.where(low, ref[:, pl.ds(base, LANES)], ref[:, pl.ds(after, LANES)]), back, 1)
                    for ref in (x_ref, c_ref)
                ]
            )
        head = lane < tab[2, j]
        out_ref[j, 0:16, :] = jnp.where(head, both[0][0], both[1][0])
        out_ref[j, 16:32, :] = jnp.where(head, both[0][1], both[1][1])
        return carry

    lax.fori_loop(0, owners, owner, 0, unroll=OWNERS_AT_ONCE)
    tell.wait()


def unpack_kernel(table, got_ref, out_ref, wide):
    users = table.shape[0] // 4
    lane = lax.broadcasted_iota(jnp.int32, (16, LANES), 1)

    def user(u, carry):
        off = table[u]
        own = table[3 * users + u]
        inside = off & (LANES - 1)
        base = pl.multiple_of(off - inside, LANES)
        turn = (inside - table[users + u]) & (LANES - 1)
        moved = pltpu.roll(got_ref[own >> 1, pl.ds(pl.multiple_of((own & 1) * 16, 16), 16), :], turn, 1).astype(F32)
        end = inside + table[2 * users + u]
        pltpu.store(wide.at[:, pl.ds(base, LANES)], moved, mask=(lane >= inside) & (lane < end))
        pltpu.store(wide.at[:, pl.ds(base + LANES, LANES)], moved, mask=lane < end - LANES)
        return carry

    lax.fori_loop(0, users, user, 0, unroll=MOVES_AT_ONCE)
    out_ref[...] = wide[:, : out_ref.shape[1]].astype(BF)


def sigmoid(v):
    return 0.5 * jnp.tanh(0.5 * v) + 0.5


def norm_parts(v):
    center = v - jnp.mean(v, axis=-1, keepdims=True)
    rstd = lax.rsqrt(jnp.mean(center * center, axis=-1, keepdims=True) + EPS)
    return center * rstd, rstd


def norm_back(hat, rstd, d):
    return rstd * (d - jnp.mean(d, axis=-1, keepdims=True) - hat * jnp.mean(d * hat, axis=-1, keepdims=True))


def column_chunks(w_hbm, w_ref, sems, order):
    per = w_hbm.shape[1] // len(order)

    def copy(i):
        part = pl.ds(order[i] * per, per)
        return pltpu.make_async_copy(w_hbm.at[:, part], w_ref.at[:, part], sems.at[i])

    def start(i):
        if i < len(order):
            copy(i).start()

    def wait(i):
        copy(i).wait()
        start(i + IN_FLIGHT)
        return slice(order[i] * per, (order[i] + 1) * per)

    for i in range(IN_FLIGHT):
        start(i)
    return wait


def forward_kernel(mine_hbm, rc_ref, w_hbm, acts_ref, slope_ref, wts_ref, wslope_ref, ahat_ref, arstd_ref, keep_ref, swap_ref, w_in, mine, sems):
    width = rc_ref.shape[0] * 16
    rows = rc_ref.shape[2]
    tell = pltpu.make_async_copy(mine_hbm.at[pl.ds(0, mine.shape[0])], mine, sems.at[CHUNKS])
    tell.start()
    order = HALVES[0] + HALVES[1] + GATES
    wait = column_chunks(w_hbm, w_in, sems, order)
    x = rc_ref[:, 0:16, :].reshape(width, rows).T
    normed = norm_parts(x.astype(F32))[0].astype(BF)
    query = lax.broadcasted_iota(jnp.int32, (rows, rows), 0)
    key = lax.broadcasted_iota(jnp.int32, (rows, rows), 1)
    tell.wait()
    first = mine[0:1, :]
    allowed = ((query < first) == (key < first)) & (key <= query)
    each = width // HEADS
    scale = float(each) ** -0.5
    attended = []

    def project(*chunks):
        for part in [wait(i) for i in chunks]:
            pre = dot(normed, w_in[:, part], 1, 0)
            gate = sigmoid(pre)
            act = pre * gate
            acts_ref[:, part] = act.astype(BF)
            slope_ref[:, part] = (gate + act * (1.0 - gate)).astype(BF)

    for half in range(2):
        project(*((0, 1, 2), (3, 4, 5, 6, 7))[half])
        for h in range(half * HEADS // 2, (half + 1) * HEADS // 2):
            v = acts_ref[:, width + h * each : width + (h + 1) * each]
            q = acts_ref[:, 2 * width + h * each : 2 * width + (h + 1) * each]
            k = acts_ref[:, 3 * width + h * each : 3 * width + (h + 1) * each]
            scores = dot(q, k, 1, 1) * scale
            gate = sigmoid(scores)
            weight = scores * gate
            kept = jnp.where(allowed, weight, 0.0).astype(BF)
            wts_ref[h] = kept
            wslope_ref[h] = jnp.where(allowed, (gate + weight * (1.0 - gate)) * scale, 0.0).astype(BF)
            attended.append(dot(kept, v, 1, 0))
    hat, rstd = norm_parts(jnp.concatenate(attended, axis=1))
    ahat_ref[...] = hat
    arstd_ref[...] = jnp.broadcast_to(rstd, arstd_ref.shape)
    mixed = (hat * acts_ref[:, :width].astype(F32)).astype(BF).T.reshape(32, 2, 16, rows)
    even = core_index() == 0
    keep_ref[...] = jnp.where(even, mixed[:, 0], mixed[:, 1]).reshape(width // 2, rows)
    swap_ref[: width // 2] = jnp.where(even, mixed[:, 1], mixed[:, 0]).reshape(width // 2, rows)
    swap_ref[width // 2 :] = rc_ref[:, 16:32, :].reshape(width, rows)


def mixed_grad_kernel(rc_ref, w_out_ref, d_mixed_ref):
    cots = rc_ref[:, 16:32, :].reshape(-1, LANES)
    d_mixed_ref[...] = dot(cots, w_out_ref[...], 0, 1).astype(BF)


def product_kernel(rc_ref, own_ref, got_ref, order_hbm, *out_refs):
    half = own_ref.shape[0]
    up = 2 * (lax.axis_index("rep") & 1)
    right = (lax.axis_index("col") >> 1) & 1
    mixed = jnp.concatenate([own_ref[...], got_ref[:half]], axis=1)
    for to, out in zip((up + right, 3 - up - right, 2 - up + right, up + 1 - right), out_refs):
        left_part = rc_ref[pl.ds(to * 16, 16), 16:32, :].reshape(256, LANES)
        right_part = got_ref[pl.ds(pl.multiple_of(half + to * 256, 256), 256), :]
        term = dot(mixed, jnp.concatenate([left_part, right_part], axis=1), 1, 1).astype(BF)
        out[:, 0:16, :] = term[:, :LANES].reshape(32, 16, LANES)
        out[:, 16:32, :] = term[:, LANES:].reshape(32, 16, LANES)


def backward_kernel(rc_ref, d_mixed_ref, acts_ref, slope_ref, wts_ref, wslope_ref, ahat_ref, arstd_ref, w_in, keep_ref, swap_ref, d_pre):
    width = rc_ref.shape[0] * 16
    rows = rc_ref.shape[2]
    d_mixed = d_mixed_ref[...].astype(F32)
    hat = ahat_ref[...]
    d_pre[:, :width] = ((d_mixed * hat) * slope_ref[:, :width].astype(F32)).astype(BF)
    d_att = norm_back(hat, arstd_ref[:, 0:1], d_mixed * acts_ref[:, :width].astype(F32)).astype(BF)
    each = width // HEADS
    for h in range(HEADS):
        vs = slice(width + h * each, width + (h + 1) * each)
        qs = slice(2 * width + h * each, 2 * width + (h + 1) * each)
        ks = slice(3 * width + h * each, 3 * width + (h + 1) * each)
        da = d_att[:, h * each : (h + 1) * each]
        d_weight = dot(da, acts_ref[:, vs], 1, 1)
        d_score = (d_weight * wslope_ref[h].astype(F32)).astype(BF)
        d_pre[:, vs] = (dot(wts_ref[h], da, 0, 0) * slope_ref[:, vs].astype(F32)).astype(BF)
        d_pre[:, qs] = (dot(d_score, acts_ref[:, ks], 1, 0) * slope_ref[:, qs].astype(F32)).astype(BF)
        d_pre[:, ks] = (dot(d_score, acts_ref[:, qs], 0, 0) * slope_ref[:, ks].astype(F32)).astype(BF)
    d_normed = dot(d_pre[...], w_in[...], 1, 1)
    cots = rc_ref[:, 16:32, :].reshape(width, rows).T
    x = rc_ref[:, 0:16, :].reshape(width, rows).T
    normed, rstd = norm_parts(x.astype(F32))
    grad = norm_back(normed, rstd, d_normed) + cots.astype(F32)
    grad = grad.astype(BF).T.reshape(32, 2, 16, rows)
    even = core_index() == 0
    keep_ref[...] = jnp.where(even, grad[:, 0], grad[:, 1])
    swap_ref[...] = jnp.where(even, grad[:, 1], grad[:, 0])


def merge_kernel(keep_ref, swapped_ref, *refs):
    out_ref = refs[-1]
    core = core_index()
    out_ref[:, pl.ds(pl.multiple_of(core * 16, 16), 16), :] = keep_ref[...]
    out_ref[:, pl.ds(pl.multiple_of((1 - core) * 16, 16), 16), :] = swapped_ref[...]
    total = refs[0][...].astype(F32)
    for part in refs[1:-1]:
        total += part[...].astype(F32)
    out_ref[:, 32:64, :] = total.astype(BF)


def last_sum_kernel(got_ref, out_ref):
    for side in range(2):
        total = got_ref[side, 32:64, :].astype(F32)
        for i in range(side + 2, got_ref.shape[0], 2):
            total += got_ref[i, 32:64, :].astype(F32)
        out_ref[:, 2 * side * LANES : (2 * side + 1) * LANES] = total[0:16]
        out_ref[:, (2 * side + 1) * LANES : (2 * side + 2) * LANES] = total[16:32]


def join_kernel(mine_ref, three_ref, two_ref, one_ref, out_ref):
    half = mine_ref.shape[1]
    up = lax.axis_index("rep") & 1
    out_ref[:, pl.ds(pl.multiple_of(up * half, half), half)] = mine_ref[...] + two_ref[...]
    out_ref[:, pl.ds(pl.multiple_of((1 - up) * half, half), half)] = one_ref[...] + three_ref[...]


def partners(along_x, along_rep):
    pairs = []
    for i in range(64):
        way = (1, 3)[i % 2]
        for y in range(4):
            to = i ^ (2 * way if along_x else 0), y ^ (way if along_rep else 0)
            pairs.append((i * 4 + y, to[0] * 4 + to[1]))
    return pairs


def per_device(looked, cotangent, w_in, w_out, lengths, owner):
    cols = lax.axis_size("col")
    events, mine_cols = looked.shape
    width = w_out.shape[0]
    rows = events // cols
    users = lengths.shape[0]
    send, table, first = pl.pallas_call(
        pack_kernel,
        out_shape=(
            shape((cols, 2 * mine_cols, rows)),
            shape((4 * users,), jnp.int32),
            shape((16384, LANES), jnp.int32),
        ),
        in_specs=[HBM] * 4,
        out_specs=(VMEM, SMEM, HBM),
        scratch_shapes=[
            pltpu.VMEM((mine_cols, events), BF),
            pltpu.VMEM((mine_cols, events), BF),
            pltpu.SMEM((4, cols), jnp.int32),
            pltpu.SMEM((cols,), jnp.int32),
            pltpu.VMEM((8, LANES), jnp.int32),
            pltpu.SemaphoreType.DMA((5,)),
        ],
        compiler_params=params(60),
    )(lengths, owner, looked.T, cotangent.T)
    packed = lax.all_to_all(send, "col", split_axis=0, concat_axis=0, tiled=True)
    acts, slope, wts, wslope, ahat, arstd, keep, swap, w_near = pl.pallas_call(
        forward_kernel,
        out_shape=(
            shape((rows, 4 * width)),
            shape((rows, 4 * width)),
            shape((HEADS, rows, rows)),
            shape((HEADS, rows, rows)),
            shape((rows, width), F32),
            shape((rows, LANES), F32),
            shape((width // 2, rows)),
            shape((width + width // 2, rows)),
            shape(w_in.shape),
        ),
        in_specs=[HBM, VMEM, HBM],
        scratch_shapes=[pltpu.VMEM((8, LANES), jnp.int32), pltpu.SemaphoreType.DMA((CHUNKS + 1,))],
        compiler_params=params(FWD_MIB),
    )(first, packed, w_in)
    other_core = [(i, i ^ 1) for i in range(cols)]
    got = lax.ppermute(swap, "col", other_core)
    d_mixed = pl.pallas_call(mixed_grad_kernel, out_shape=shape((rows, width)), compiler_params=params(16))(packed, w_out)
    block = (cols // 2, 2 * mine_cols, LANES)
    terms = pl.pallas_call(
        product_kernel,
        out_shape=[shape(block)] * 4,
        in_specs=[VMEM, VMEM, VMEM, ANY],
        compiler_params=params(16),
    )(packed, keep, got, d_mixed)
    ways = (True, True), (False, True), (True, False)
    terms = [terms[0]] + [lax.ppermute(t, ("col", "rep"), partners(*way)) for t, way in zip(terms[1:], ways)]
    grad, swap = pl.pallas_call(
        backward_kernel,
        out_shape=[shape((cols // 2, mine_cols, rows))] * 2,
        in_specs=[VMEM] * 9,
        scratch_shapes=[pltpu.VMEM((rows, 4 * width), BF)],
        compiler_params=params(16),
    )(packed, d_mixed, acts, slope, wts, wslope, ahat, arstd, w_near)
    swapped = lax.ppermute(swap, "col", other_core)
    merged = pl.pallas_call(
        merge_kernel,
        out_shape=shape((cols // 2, 4 * mine_cols, rows)),
        in_specs=[VMEM] * 6,
        compiler_params=params(16),
    )(grad, swapped, *terms)
    same_core = [list(range(core, cols, 2)) for core in range(2)]
    back = lax.all_to_all(merged, "col", split_axis=0, concat_axis=0, axis_index_groups=same_core, tiled=True)
    mine = pl.pallas_call(last_sum_kernel, out_shape=shape((mine_cols, width // 2), F32), compiler_params=params(16))(back)
    three, two, one = [lax.ppermute(mine, "rep", [(i, i ^ k) for i in range(4)]) for k in (3, 2, 1)]
    d_looked = pl.pallas_call(
        unpack_kernel,
        out_shape=shape((mine_cols, events)),
        in_specs=[SMEM, VMEM],
        scratch_shapes=[pltpu.VMEM((mine_cols, events + LANES), F32)],
        compiler_params=params(16),
    )(table, back)
    d_w_out = pl.pallas_call(
        join_kernel, out_shape=shape((mine_cols, width), F32), in_specs=[VMEM] * 4, compiler_params=params(16)
    )(mine, three, two, one)
    return (d_looked.T, d_w_out)


def solution(mesh):
    placed = (P("rep", "col"), P("rep", "col"), P(), P(), P("rep"), P("rep"))
    return jax.shard_map(
        per_device,
        mesh=mesh,
        in_specs=placed,
        out_specs=(P("rep", "col"), P("col", None)),
        check_vma=False,
    )
```

```python
import functools

import jax
import jax.numpy as jnp
from jax import lax
from jax.experimental import pallas as pl
from jax.experimental.pallas import tpu as pltpu
from jax.sharding import PartitionSpec as P

HEADS = 8
EPS = 1e-05
BF = jnp.bfloat16
F32 = jnp.float32
LANES = 128
CHUNKS = 8
IN_FLIGHT = 8
HALVES = ((2, 4, 6), (3, 5, 7))
GATES = (0, 1)
FWD_MIB = 38
USERS_AT_ONCE = 32
OWNERS_AT_ONCE = 8
MOVES_AT_ONCE = 16

SMEM = pl.BlockSpec(memory_space=pltpu.SMEM)
VMEM = pl.BlockSpec(memory_space=pltpu.VMEM)
ANY = pl.BlockSpec(memory_space=pl.ANY)
HBM = pl.BlockSpec(memory_space=pltpu.HBM)


def params(mib):
    return pltpu.CompilerParams(vmem_limit_bytes=mib << 20)


def core_index():
    return lax.axis_index("col") & 1


def shape(dims, dtype=BF):
    return jax.ShapeDtypeStruct(dims, dtype)


def dot(a, b, ca, cb):
    return lax.dot_general(a, b, (((ca,), (cb,)), ((), ())), preferred_element_type=F32)


def pack_kernel(len_hbm, own_hbm, x_hbm, c_hbm, out_ref, table, mine_hbm, x_ref, c_ref, tab, seen, mine, sems):
    users = len_hbm.shape[0]
    lens, owns = table.at[pl.ds(2 * users, users)], table.at[pl.ds(3 * users, users)]
    copies = [
        pltpu.make_async_copy(src, dst, sems.at[i])
        for i, (src, dst) in enumerate(((len_hbm, lens), (own_hbm, owns), (x_hbm, x_ref), (c_hbm, c_ref)))
    ]
    for copy in copies:
        copy.start()
    owners = users // 2
    last = x_ref.shape[1] - LANES
    for j in range(owners):
        seen[j] = 0
    copies[0].wait()
    copies[1].wait()

    def user(u, off):
        own = table[3 * users + u]
        length = table[2 * users + u]
        second = seen[own]
        seen[own] = 1
        start = second * (LANES - length)
        table[u] = off
        table[users + u] = start
        tab[second, own] = off - start
        tab[2 + second, own] = length
        return off + length

    lax.fori_loop(0, users, user, 0, unroll=USERS_AT_ONCE)
    mine[...] = jnp.full(mine.shape, tab[2, lax.axis_index("col")], jnp.int32)
    tell = pltpu.make_async_copy(mine, mine_hbm.at[pl.ds(0, mine.shape[0])], sems.at[4])
    tell.start()
    copies[2].wait()
    copies[3].wait()
    lane = lax.broadcasted_iota(jnp.int32, (16, LANES), 1)

    def owner(j, carry):
        both = []
        for k in range(2):
            first = tab[k, j]
            inside = first & (LANES - 1)
            base = pl.multiple_of(first - inside, LANES)
            after = pl.multiple_of(jnp.minimum(base + LANES, last), LANES)
            back = (LANES - inside) & (LANES - 1)
            low = lane >= inside
            both.append(
                [
                    pltpu.roll(jnp.where(low, ref[:, pl.ds(base, LANES)], ref[:, pl.ds(after, LANES)]), back, 1)
                    for ref in (x_ref, c_ref)
                ]
            )
        head = lane < tab[2, j]
        out_ref[j, 0:16, :] = jnp.where(head, both[0][0], both[1][0])
        out_ref[j, 16:32, :] = jnp.where(head, both[0][1], both[1][1])
        return carry

    lax.fori_loop(0, owners, owner, 0, unroll=OWNERS_AT_ONCE)
    tell.wait()


def unpack_kernel(table, got_ref, out_ref, wide):
    users = table.shape[0] // 4
    lane = lax.broadcasted_iota(jnp.int32, (16, LANES), 1)

    def user(u, carry):
        off = table[u]
        own = table[3 * users + u]
        inside = off & (LANES - 1)
        base = pl.multiple_of(off - inside, LANES)
        turn = (inside - table[users + u]) & (LANES - 1)
        moved = pltpu.roll(got_ref[own >> 1, pl.ds(pl.multiple_of((own & 1) * 16, 16), 16), :], turn, 1).astype(F32)
        end = inside + table[2 * users + u]
        pltpu.store(wide.at[:, pl.ds(base, LANES)], moved, mask=(lane >= inside) & (lane < end))
        pltpu.store(wide.at[:, pl.ds(base + LANES, LANES)], moved, mask=lane < end - LANES)
        return carry

    lax.fori_loop(0, users, user, 0, unroll=MOVES_AT_ONCE)
    out_ref[...] = wide[:, : out_ref.shape[1]].astype(BF)


def sigmoid(v):
    return 0.5 * jnp.tanh(0.5 * v) + 0.5


def norm_parts(v):
    center = v - jnp.mean(v, axis=-1, keepdims=True)
    rstd = lax.rsqrt(jnp.mean(center * center, axis=-1, keepdims=True) + EPS)
    return center * rstd, rstd


def norm_back(hat, rstd, d):
    return rstd * (d - jnp.mean(d, axis=-1, keepdims=True) - hat * jnp.mean(d * hat, axis=-1, keepdims=True))


def column_chunks(w_hbm, w_ref, sems, order):
    per = w_hbm.shape[1] // len(order)

    def copy(i):
        part = pl.ds(order[i] * per, per)
        return pltpu.make_async_copy(w_hbm.at[:, part], w_ref.at[:, part], sems.at[i])

    def start(i):
        if i < len(order):
            copy(i).start()

    def wait(i):
        copy(i).wait()
        start(i + IN_FLIGHT)
        return slice(order[i] * per, (order[i] + 1) * per)

    for i in range(IN_FLIGHT):
        start(i)
    return wait


def forward_kernel(mine_hbm, rc_ref, w_hbm, acts_ref, slope_ref, wts_ref, wslope_ref, ahat_ref, arstd_ref, keep_ref, swap_ref, w_in, mine, sems):
    width = rc_ref.shape[0] * 16
    rows = rc_ref.shape[2]
    tell = pltpu.make_async_copy(mine_hbm.at[pl.ds(0, mine.shape[0])], mine, sems.at[CHUNKS])
    tell.start()
    order = HALVES[0] + HALVES[1] + GATES
    wait = column_chunks(w_hbm, w_in, sems, order)
    x = rc_ref[:, 0:16, :].reshape(width, rows).T
    normed = norm_parts(x.astype(F32))[0].astype(BF)
    query = lax.broadcasted_iota(jnp.int32, (rows, rows), 0)
    key = lax.broadcasted_iota(jnp.int32, (rows, rows), 1)
    tell.wait()
    first = mine[0:1, :]
    allowed = ((query < first) == (key < first)) & (key <= query)
    each = width // HEADS
    scale = float(each) ** -0.5
    attended = []

    def project(*chunks):
        for part in [wait(i) for i in chunks]:
            pre = dot(normed, w_in[:, part], 1, 0)
            gate = sigmoid(pre)
            act = pre * gate
            acts_ref[:, part] = act.astype(BF)
            slope_ref[:, part] = (gate + act * (1.0 - gate)).astype(BF)

    for half in range(2):
        project(*((0, 1, 2), (3, 4, 5, 6, 7))[half])
        for h in range(half * HEADS // 2, (half + 1) * HEADS // 2):
            v = acts_ref[:, width + h * each : width + (h + 1) * each]
            q = acts_ref[:, 2 * width + h * each : 2 * width + (h + 1) * each]
            k = acts_ref[:, 3 * width + h * each : 3 * width + (h + 1) * each]
            scores = dot(q, k, 1, 1) * scale
            gate = sigmoid(scores)
            weight = scores * gate
            kept = jnp.where(allowed, weight, 0.0).astype(BF)
            wts_ref[h] = kept
            wslope_ref[h] = jnp.where(allowed, (gate + weight * (1.0 - gate)) * scale, 0.0).astype(BF)
            attended.append(dot(kept, v, 1, 0))
    hat, rstd = norm_parts(jnp.concatenate(attended, axis=1))
    ahat_ref[...] = hat
    arstd_ref[...] = jnp.broadcast_to(rstd, arstd_ref.shape)
    mixed = (hat * acts_ref[:, :width].astype(F32)).astype(BF).T.reshape(32, 2, 16, rows)
    even = core_index() == 0
    keep_ref[...] = jnp.where(even, mixed[:, 0], mixed[:, 1]).reshape(width // 2, rows)
    swap_ref[: width // 2] = jnp.where(even, mixed[:, 1], mixed[:, 0]).reshape(width // 2, rows)
    swap_ref[width // 2 :] = rc_ref[:, 16:32, :].reshape(width, rows)


def mixed_grad_kernel(rc_ref, w_out_ref, d_mixed_ref):
    cots = rc_ref[:, 16:32, :].reshape(-1, LANES)
    d_mixed_ref[...] = dot(cots, w_out_ref[...], 0, 1).astype(BF)


def product_kernel(rc_ref, own_ref, got_ref, order_hbm, *out_refs):
    half = own_ref.shape[0]
    up = 2 * (lax.axis_index("rep") & 1)
    right = (lax.axis_index("col") >> 1) & 1
    mixed = jnp.concatenate([own_ref[...], got_ref[:half]], axis=1)
    for to, out in zip((up + right, 3 - up - right, 2 - up + right, up + 1 - right), out_refs):
        left_part = rc_ref[pl.ds(to * 16, 16), 16:32, :].reshape(256, LANES)
        right_part = got_ref[pl.ds(pl.multiple_of(half + to * 256, 256), 256), :]
        term = dot(mixed, jnp.concatenate([left_part, right_part], axis=1), 1, 1).astype(BF)
        out[:, 0:16, :] = term[:, :LANES].reshape(32, 16, LANES)
        out[:, 16:32, :] = term[:, LANES:].reshape(32, 16, LANES)


def backward_kernel(rc_ref, d_mixed_ref, acts_ref, slope_ref, wts_ref, wslope_ref, ahat_ref, arstd_ref, w_in, keep_ref, swap_ref, d_pre):
    width = rc_ref.shape[0] * 16
    rows = rc_ref.shape[2]
    d_mixed = d_mixed_ref[...].astype(F32)
    hat = ahat_ref[...]
    d_pre[:, :width] = ((d_mixed * hat) * slope_ref[:, :width].astype(F32)).astype(BF)
    d_att = norm_back(hat, arstd_ref[:, 0:1], d_mixed * acts_ref[:, :width].astype(F32)).astype(BF)
    each = width // HEADS
    for h in range(HEADS):
        vs = slice(width + h * each, width + (h + 1) * each)
        qs = slice(2 * width + h * each, 2 * width + (h + 1) * each)
        ks = slice(3 * width + h * each, 3 * width + (h + 1) * each)
        da = d_att[:, h * each : (h + 1) * each]
        d_weight = dot(da, acts_ref[:, vs], 1, 1)
        d_score = (d_weight * wslope_ref[h].astype(F32)).astype(BF)
        d_pre[:, vs] = (dot(wts_ref[h], da, 0, 0) * slope_ref[:, vs].astype(F32)).astype(BF)
        d_pre[:, qs] = (dot(d_score, acts_ref[:, ks], 1, 0) * slope_ref[:, qs].astype(F32)).astype(BF)
        d_pre[:, ks] = (dot(d_score, acts_ref[:, qs], 0, 0) * slope_ref[:, ks].astype(F32)).astype(BF)
    d_normed = dot(d_pre[...], w_in[...], 1, 1)
    cots = rc_ref[:, 16:32, :].reshape(width, rows).T
    x = rc_ref[:, 0:16, :].reshape(width, rows).T
    normed, rstd = norm_parts(x.astype(F32))
    grad = norm_back(normed, rstd, d_normed) + cots.astype(F32)
    grad = grad.astype(BF).T.reshape(32, 2, 16, rows)
    even = core_index() == 0
    keep_ref[...] = jnp.where(even, grad[:, 0], grad[:, 1])
    swap_ref[...] = jnp.where(even, grad[:, 1], grad[:, 0])


def merge_kernel(keep_ref, swapped_ref, *refs):
    out_ref = refs[-1]
    core = core_index()
    out_ref[:, pl.ds(pl.multiple_of(core * 16, 16), 16), :] = keep_ref[...]
    out_ref[:, pl.ds(pl.multiple_of((1 - core) * 16, 16), 16), :] = swapped_ref[...]
    total = refs[0][...].astype(F32)
    for part in refs[1:-1]:
        total += part[...].astype(F32)
    out_ref[:, 32:64, :] = total.astype(BF)


def last_sum_kernel(got_ref, out_ref):
    for side in range(2):
        total = got_ref[side, 32:64, :].astype(F32)
        for i in range(side + 2, got_ref.shape[0], 2):
            total += got_ref[i, 32:64, :].astype(F32)
        out_ref[:, 2 * side * LANES : (2 * side + 1) * LANES] = total[0:16]
        out_ref[:, (2 * side + 1) * LANES : (2 * side + 2) * LANES] = total[16:32]


def join_kernel(mine_ref, two_ref, three_ref, one_ref, out_ref):
    half = mine_ref.shape[1]
    up = lax.axis_index("rep") & 1
    out_ref[:, pl.ds(pl.multiple_of(up * half, half), half)] = mine_ref[...] + two_ref[...]
    out_ref[:, pl.ds(pl.multiple_of((1 - up) * half, half), half)] = one_ref[...] + three_ref[...]


def partners(along_x, along_rep):
    pairs = []
    for i in range(64):
        way = (1, 3)[i % 2]
        for y in range(4):
            to = i ^ (2 * way if along_x else 0), y ^ (way if along_rep else 0)
            pairs.append((i * 4 + y, to[0] * 4 + to[1]))
    return pairs


def per_device(looked, cotangent, w_in, w_out, lengths, owner):
    cols = lax.axis_size("col")
    events, mine_cols = looked.shape
    width = w_out.shape[0]
    rows = events // cols
    users = lengths.shape[0]
    send, table, first = pl.pallas_call(
        pack_kernel,
        out_shape=(
            shape((cols, 2 * mine_cols, rows)),
            shape((4 * users,), jnp.int32),
            shape((16384, LANES), jnp.int32),
        ),
        in_specs=[HBM] * 4,
        out_specs=(VMEM, SMEM, HBM),
        scratch_shapes=[
            pltpu.VMEM((mine_cols, events), BF),
            pltpu.VMEM((mine_cols, events), BF),
            pltpu.SMEM((4, cols), jnp.int32),
            pltpu.SMEM((cols,), jnp.int32),
            pltpu.VMEM((8, LANES), jnp.int32),
            pltpu.SemaphoreType.DMA((5,)),
        ],
        compiler_params=params(60),
    )(lengths, owner, looked.T, cotangent.T)
    packed = lax.all_to_all(send, "col", split_axis=0, concat_axis=0, tiled=True)
    acts, slope, wts, wslope, ahat, arstd, keep, swap, w_near = pl.pallas_call(
        forward_kernel,
        out_shape=(
            shape((rows, 4 * width)),
            shape((rows, 4 * width)),
            shape((HEADS, rows, rows)),
            shape((HEADS, rows, rows)),
            shape((rows, width), F32),
            shape((rows, LANES), F32),
            shape((width // 2, rows)),
            shape((width + width // 2, rows)),
            shape(w_in.shape),
        ),
        in_specs=[HBM, VMEM, HBM],
        scratch_shapes=[pltpu.VMEM((8, LANES), jnp.int32), pltpu.SemaphoreType.DMA((CHUNKS + 1,))],
        compiler_params=params(FWD_MIB),
    )(first, packed, w_in)
    other_core = [(i, i ^ 1) for i in range(cols)]
    got = lax.ppermute(swap, "col", other_core)
    d_mixed = pl.pallas_call(mixed_grad_kernel, out_shape=shape((rows, width)), compiler_params=params(16))(packed, w_out)
    block = (cols // 2, 2 * mine_cols, LANES)
    terms = pl.pallas_call(
        product_kernel,
        out_shape=[shape(block)] * 4,
        in_specs=[VMEM, VMEM, VMEM, ANY],
        compiler_params=params(16),
    )(packed, keep, got, d_mixed)
    ways = (True, True), (False, True), (True, False)
    terms = [terms[0]] + [lax.ppermute(t, ("col", "rep"), partners(*way)) for t, way in zip(terms[1:], ways)]
    grad, swap = pl.pallas_call(
        backward_kernel,
        out_shape=[shape((cols // 2, mine_cols, rows))] * 2,
        in_specs=[VMEM] * 9,
        scratch_shapes=[pltpu.VMEM((rows, 4 * width), BF)],
        compiler_params=params(16),
    )(packed, d_mixed, acts, slope, wts, wslope, ahat, arstd, w_near)
    swapped = lax.ppermute(swap, "col", other_core)
    merged = pl.pallas_call(
        merge_kernel,
        out_shape=shape((cols // 2, 4 * mine_cols, rows)),
        in_specs=[VMEM] * 6,
        compiler_params=params(16),
    )(grad, swapped, *terms)
    same_core = [list(range(core, cols, 2)) for core in range(2)]
    back = lax.all_to_all(merged, "col", split_axis=0, concat_axis=0, axis_index_groups=same_core, tiled=True)
    mine = pl.pallas_call(last_sum_kernel, out_shape=shape((mine_cols, width // 2), F32), compiler_params=params(16))(back)
    two, three, one = [lax.ppermute(mine, "rep", [(i, i ^ k) for i in range(4)]) for k in (2, 3, 1)]
    d_looked = pl.pallas_call(
        unpack_kernel,
        out_shape=shape((mine_cols, events)),
        in_specs=[SMEM, VMEM],
        scratch_shapes=[pltpu.VMEM((mine_cols, events + LANES), F32)],
        compiler_params=params(16),
    )(table, back)
    d_w_out = pl.pallas_call(
        join_kernel, out_shape=shape((mine_cols, width), F32), in_specs=[VMEM] * 4, compiler_params=params(16)
    )(mine, two, three, one)
    return (d_looked.T, d_w_out)


def solution(mesh):
    placed = (P("rep", "col"), P("rep", "col"), P(), P(), P("rep"), P("rep"))
    return jax.shard_map(
        per_device,
        mesh=mesh,
        in_specs=placed,
        out_specs=(P("rep", "col"), P("col", None)),
        check_vma=False,
    )
```
